512 devices in a mesh: depth: 16 (over z, core), freq: 32 (over x, y).
Axes of the slice: x: 4, y: 8, z: 8, core: 2. Of those that a mesh axis runs over, the one named last changes fastest.
Arguments:
- traces: bfloat16 [16384, 128], P('freq'), may hold values from -6 to 6
- shot_of_trace: int32 [32, 512], P('freq'), may hold values from 0 to 5, never falling along the last dimension, each value on 1 to 128 neighbouring positions
- receiver_cell: int32 [32, 512], P('freq'), may hold values from 0 to 511
- slot_freq: int32 [64], P('freq'), may hold values from 0 to 63, each once
- operators: bfloat16 [16, 64, 2, 512, 512], P('depth', 'freq'), may hold values from -1 to 1
- slowness: float32 [16, 512], P('depth'), may hold values from 0.5 to 2
- image_model: float32 [16, 512], P('depth'), may hold values from -3 to 3
Outputs:
- gradient: float32 [16, 512], P('depth')
- adjoint_tops: bfloat16 [16, 64, 2, 192, 512], P('depth', 'freq')
The draws below stay inside these ranges and needn't reach their ends.
Inputs may be any that keep to these rules, and one draw needn't show every extreme that they name: `shot_of_trace`: within each row of 512 entries the numbers never fall and each of 0 to 5 appears. A program may pack these labels, and the receiver cells, several to a 32-bit word while they travel between devices. `receiver_cell`: A program may pack these labels, and the shot numbers, several to a 32-bit word while they travel between devices. `slot_freq`: each frequency number once.
All inputs are finite; a program needn't handle non-finite values.
Results may differ from the reference program's by a relative error of at most 0.023.
Values may be sent and summed in bfloat16 or wider, within the bound.
A program may use at most 192 MiB of HBM per device.

```python
import math
import jax
import jax.numpy as jnp
import numpy as np
from jax import lax

LATERAL = 512
STEPS = 1
SHOTS_DEV = 6
TRACE_DEV = 512
FREQS = 64
SHOTS = 192
TRACES = 16384
DEPTHS = 16
N_DEPTH = 16
N_FREQ = 32


def draw_operators(key, part):
    key = jax.random.fold_in(key, 11)
    spread = 0.2 / math.sqrt(LATERAL)
    identity = jnp.eye(LATERAL, dtype=jnp.float32)

    def one_depth(depth_index):
        depth_key = jax.random.fold_in(key, depth_index)
        angle_key, other_key = jax.random.split(depth_key)
        diagonal_angle = jax.random.uniform(angle_key, (FREQS, LATERAL), jnp.float32, -math.pi, math.pi)
        offdiag = jax.random.truncated_normal(other_key, -3.0, 3.0, (FREQS, 2, LATERAL, LATERAL), jnp.float32)
        diagonal_part = jnp.stack([jnp.cos(diagonal_angle), jnp.sin(diagonal_angle)], axis=1)[..., None] * identity
        matrices = (diagonal_part + offdiag * spread * (1.0 - identity)) * (1.0 / math.sqrt(1.08))
        return matrices.astype(jnp.bfloat16)
    return lax.map(one_depth, jnp.arange(DEPTHS, dtype=jnp.int32))


def place_ends(result, own_key, smallest, largest):
    index_at = [jax.random.randint(jax.random.fold_in(own_key, axis), (), 0, length) for axis, length in enumerate(result.shape)]
    main_axis = result.shape.index(max(result.shape))
    next_to = index_at[:main_axis] + [(index_at[main_axis] + 1) % result.shape[main_axis]] + index_at[main_axis + 1:]
    return result.at[tuple(index_at)].set(smallest).at[tuple(next_to)].set(largest)


def shard_levels(own_key, extent, cuts, smallest, top_value):
    level = 1.0
    for dim, shards_of in cuts:
        draws = jax.random.uniform(jax.random.fold_in(jax.random.fold_in(own_key, 6), dim), (shards_of,), jnp.float32, smallest / len(cuts), top_value / len(cuts))
        level = level * jnp.repeat(jnp.exp(draws), extent[dim] // shards_of).reshape((-1,) + (1,) * (len(extent) - 1 - dim))
    return level


def split_up(count, total, most, lean):
    loads = [(1 << 20) // math.isqrt(grade ** lean) + 1 for grade in range(2, count + 1)]
    spare, given = total - most - (count - 1), [1] * (count - 1)
    while spare > 0:
        free = [i for i in range(count - 1) if given[i] < most]
        whole, budget = sum([loads[i] for i in free]), spare
        for i in free:
            more = min(most - given[i], max(1, budget * loads[i] // whole), spare)
            given[i] = given[i] + more
            spare = spare - more
    return np.array([most] + given)


def uneven_parts(key, count, total, reach, skew):
    if count == 2:
        one = jax.random.randint(key, (), max(1, total - reach), min(reach, total - 1) + 1)
        return jnp.stack([one, total - one])
    sizes = jnp.asarray(split_up(count, total, reach, skew), jnp.int32)
    twos = (count - 1) // 2
    source_of, sink = sizes[1:1 + 2 * twos:2], sizes[2:2 + 2 * twos:2]
    room = jnp.minimum(source_of - 1, reach - sink)
    moved = jax.random.randint(jax.random.fold_in(key, 1), (twos,), 0, 1 << 20) % (room + 1)
    sizes = sizes.at[1:1 + 2 * twos:2].set(source_of - moved).at[2:2 + 2 * twos:2].set(sink + moved)
    return sizes[jax.random.permutation(jax.random.fold_in(key, 2), count)]


def noise(rng, shape, scale, limit, cuts=(), kind=jnp.bfloat16):
    loudness = shard_levels(rng, shape, cuts, -0.22, 0.18) if cuts else 1.0
    drawn = jax.random.normal(rng, shape, jnp.float32) * scale * loudness
    return jnp.minimum(jnp.maximum(drawn, -limit), limit).astype(kind)


def setup_inputs(seed: int = 0) -> dict:
    keys = jax.random.split(jax.random.key(seed), 8)
    traces = noise(keys[0], (TRACES, 2 * FREQS), 1.0, 6.0, ((0, 32),))
    shot_of_trace = jax.vmap(lambda own: jnp.searchsorted(jnp.cumsum(uneven_parts(own, SHOTS_DEV, TRACE_DEV, min(TRACE_DEV, TRACE_DEV * 3 // (2 * SHOTS_DEV)), 1)), jnp.arange(TRACE_DEV), side="right"))(jax.random.split(keys[1], N_FREQ)).reshape((N_FREQ, TRACE_DEV)).astype(jnp.int32)
    receiver_cell = place_ends(jax.random.randint(keys[2], (N_FREQ, TRACE_DEV), 0, LATERAL), jax.random.fold_in(keys[2], 1), 0, LATERAL - 1).astype(jnp.int32)
    slot_freq = jax.random.permutation(keys[3], FREQS).astype(jnp.int32)
    operators = draw_operators(jax.random.fold_in(keys[7], 71), 0)
    slowness = jnp.clip(jnp.exp(math.log(2.0) - 1.3862944 * jax.random.uniform(keys[5], (DEPTHS, LATERAL), jnp.float32) ** shard_levels(keys[5], (DEPTHS, LATERAL), ((0, 16),), -0.2, 0.2)), 0.5, 2.0)
    image_model = noise(keys[6], (DEPTHS, LATERAL), 0.5, 3.0, ((0, 16),), jnp.float32)
    return dict(traces=traces, shot_of_trace=shot_of_trace, receiver_cell=receiver_cell, slot_freq=slot_freq, operators=operators, slowness=slowness, image_model=image_model)


def continue_down(wavefield, matrices, cosines, sine_values):
    shifted_list = []
    for level_index in range(STEPS):
        real_part = cosines[level_index] * wavefield[0] - sine_values[level_index] * wavefield[1]
        imag_part = cosines[level_index] * wavefield[1] + sine_values[level_index] * wavefield[0]
        shifted = jnp.stack([real_part, imag_part]).astype(jnp.bfloat16)
        shifted_list.append(shifted)
        mat_real = matrices[level_index, 0].T
        mat_imag = matrices[level_index, 1].T
        new_real = jnp.dot(shifted[0], mat_real, preferred_element_type=jnp.float32) - jnp.dot(shifted[1], mat_imag, preferred_element_type=jnp.float32)
        new_imag = jnp.dot(shifted[0], mat_imag, preferred_element_type=jnp.float32) + jnp.dot(shifted[1], mat_real, preferred_element_type=jnp.float32)
        wavefield = jnp.stack([new_real, new_imag])
    return wavefield, jnp.stack(shifted_list)


def continue_up(adjoint, matrices, cosines, sine_values, shifted_all, model_rows):
    image_terms = [None] * STEPS
    for level_index in reversed(range(STEPS)):
        shifted = shifted_all[level_index].astype(jnp.float32)
        source = adjoint + model_rows[level_index] * shifted
        image_terms[level_index] = jnp.sum(shifted[0] * source[0] + shifted[1] * source[1], axis=0)
        rounded = source.astype(jnp.bfloat16)
        mat_real = matrices[level_index, 0]
        mat_imag = matrices[level_index, 1]
        back_real = jnp.dot(rounded[0], mat_real, preferred_element_type=jnp.float32) + jnp.dot(rounded[1], mat_imag, preferred_element_type=jnp.float32)
        back_imag = jnp.dot(rounded[1], mat_real, preferred_element_type=jnp.float32) - jnp.dot(rounded[0], mat_imag, preferred_element_type=jnp.float32)
        adjoint = jnp.stack([cosines[level_index] * back_real + sine_values[level_index] * back_imag,
                             cosines[level_index] * back_imag - sine_values[level_index] * back_real])
    return adjoint, jnp.stack(image_terms)


def reference(traces, shot_of_trace, receiver_cell, slot_freq, operators, slowness, image_model):
    row_numbers = jnp.arange(TRACES, dtype=jnp.int32)
    shot_index = (row_numbers // TRACE_DEV) * SHOTS_DEV + shot_of_trace.reshape(-1)
    flat_index = shot_index * LATERAL + receiver_cell.reshape(-1)
    summed = jax.ops.segment_sum(traces.astype(jnp.float32), flat_index, num_segments=SHOTS * LATERAL)
    surface = summed.astype(jnp.bfloat16).reshape(SHOTS, LATERAL, FREQS, 2).transpose(2, 3, 0, 1)
    section_slowness = slowness.reshape(N_DEPTH, STEPS, LATERAL)
    section_model = image_model.reshape(N_DEPTH, STEPS, LATERAL)

    def per_slot(slot_index):
        matrices = operators[:, slot_index].reshape(N_DEPTH, STEPS, 2, LATERAL, LATERAL)
        phase_angle = 0.1 * (slot_freq[slot_index].astype(jnp.float32) + 1.0) * section_slowness
        cosines = jnp.cos(phase_angle)
        sine_values = jnp.sin(phase_angle)

        def down_step(wavefield, inputs):
            mats_here, cos_here, sin_here = inputs
            wavefield, shifted_all = continue_down(wavefield, mats_here, cos_here, sin_here)
            wavefield = lax.optimization_barrier(wavefield.astype(jnp.bfloat16)).astype(jnp.float32)
            return wavefield, shifted_all

        surface_field = surface[slot_index].astype(jnp.float32)
        ignored, shifted_sections = lax.scan(down_step, surface_field, (matrices, cosines, sine_values))

        def up_step(adjoint, inputs):
            mats_here, cos_here, sin_here, shifted_here, model_here = inputs
            adjoint, image_terms = continue_up(adjoint, mats_here, cos_here, sin_here, shifted_here, model_here)
            rounded = lax.optimization_barrier(adjoint.astype(jnp.bfloat16))
            return rounded.astype(jnp.float32), (rounded, image_terms)

        empty_adjoint = jnp.zeros((2, SHOTS, LATERAL), jnp.float32)
        ignored, (top_fields, image_terms) = lax.scan(
            up_step, empty_adjoint, (matrices, cosines, sine_values, shifted_sections, section_model), reverse=True)
        return top_fields, image_terms

    top_fields, image_terms = lax.map(per_slot, jnp.arange(FREQS, dtype=jnp.int32))
    gradient = jnp.sum(image_terms, axis=0).reshape(DEPTHS, LATERAL) / (FREQS * SHOTS)
    return gradient, jnp.transpose(top_fields, (1, 0, 2, 3, 4))
```

```python
import functools

import jax
import jax.numpy as jnp
from jax import lax
from jax.experimental import pallas as pl
from jax.experimental.pallas import tpu as pltpu
from jax.sharding import PartitionSpec as P

MESH = pl.DeviceIdType.MESH
SHOTS_DEV = 6
SH = 32
F32 = jnp.float32
BF16 = jnp.bfloat16


def product(rows, matrix):
    return jnp.dot(rows, matrix, preferred_element_type=F32)


def lanes(tile, row, width):
    return jnp.concatenate([tile[4 * q + row : 4 * q + row + 1] for q in range(width // 128)], axis=1)


def kernel(
    n_depth,
    n_freq,
    slot_ref,
    traces_ref,
    shot_ref,
    cell_ref,
    slow_ref,
    model_ref,
    oper_ref,
    grad_ref,
    tops_ref,
    opn,
    opt,
    par,
    cosines,
    sines,
    outbox,
    inbox,
    din,
    dout,
    vbuf,
    uin,
    abuf,
    gacc,
    gsend,
    gbox,
    gpair,
    load_sem,
    core_send,
    core_recv,
    box_send,
    box_recv,
    down_send,
    down_recv,
    up_send,
    up_recv,
    tops_local,
    tops_send,
    tops_recv,
    g_send,
    g_recv,
):
    d = lax.axis_index("depth")
    f = lax.axis_index("freq")
    z = d // 2
    c = d % 2
    last = n_depth // 2 - 1
    partner = {"depth": z * 2 + (1 - c)}
    below = {"depth": (d + 2) % n_depth}
    above = {"depth": (d + n_depth - 2) % n_depth}
    chunks = din.shape[0]
    lateral = din.shape[-1]

    barrier = pltpu.get_barrier_semaphore()
    for neighbour in (partner, below, above):
        pl.semaphore_signal(barrier, inc=1, device_id=neighbour, device_id_type=MESH)

    @pl.loop(1, n_freq)
    def _(k):
        pl.semaphore_signal(barrier, inc=1, device_id={"freq": (f + k) % n_freq}, device_id_type=MESH)

    own_copy = pltpu.make_async_copy(oper_ref.at[0, c], opn.at[c], load_sem)
    own_copy.start()

    row8 = lax.broadcasted_iota(jnp.int32, (8, lateral), 0)
    par[c] = jnp.where(row8 == 0, slow_ref[...], model_ref[...])

    @pl.when(z == 0)
    def _():
        rows = outbox.shape[0] * 16
        row = lax.broadcasted_iota(jnp.int32, (rows, 128), 0)
        column = lax.broadcasted_iota(jnp.int32, (rows, 128), 1)
        group, place = row // 16, row % 16
        kind, piece = place % 4, place // 4
        wanted = jnp.where(kind < 2, group * 4 + 2 * c + kind, -1)
        total = jnp.zeros((rows, 128), F32)
        for q in range(4):
            select = jnp.where((column == wanted) & (piece == q), 1.0, 0.0).astype(BF16)
            total += lax.dot_general(
                select,
                traces_ref[128 * q : 128 * (q + 1), :],
                (((1,), (1,)), ((), ())),
                preferred_element_type=F32,
            )
        shot = shot_ref[...]
        cell = cell_ref[...]
        first = (shot * 4 + cell // 128).astype(F32)
        second = (cell % 128).astype(F32)
        row16 = lax.broadcasted_iota(jnp.int32, (16, 128), 0)
        label = jnp.zeros((16, 128), F32)
        for q in range(4):
            label = jnp.where(row16 == 4 * q + 2, first[:, 128 * q : 128 * (q + 1)], label)
            label = jnp.where(row16 == 4 * q + 3, second[:, 128 * q : 128 * (q + 1)], label)
        filled = total.reshape(n_freq, 16, 128) + label[None]
        outbox[...] = filled.astype(BF16)
        inbox[f] = outbox[f]

    pl.semaphore_wait(barrier, n_freq + 2)

    def box_copy(k):
        return pltpu.make_async_remote_copy(
            src_ref=outbox.at[(f + k) % n_freq],
            dst_ref=inbox.at[f],
            send_sem=box_send.at[k],
            recv_sem=box_recv.at[f],
            device_id={"freq": (f + k) % n_freq},
            device_id_type=MESH,
        )

    @pl.when(z == 0)
    def _():
        @pl.loop(1, n_freq)
        def _(k):
            box_copy(k).start()

    def core_copy(source, target, index):
        return pltpu.make_async_remote_copy(
            src_ref=source,
            dst_ref=target,
            send_sem=core_send.at[index],
            recv_sem=core_recv.at[index],
            device_id=partner,
            device_id_type=MESH,
        )

    oper_copy = core_copy(oper_ref.at[0, 1 - c], opn.at[c], 0)
    par_copy = core_copy(par.at[c], par.at[c], 1)
    oper_copy.start()
    par_copy.start()
    oper_wait = core_copy(oper_ref.at[0, 1 - c], opn.at[1 - c], 0)
    par_wait = core_copy(par.at[1 - c], par.at[1 - c], 1)

    own_copy.wait()
    for p in range(2):
        opt[c, p] = opn[c, p].T
    par_wait.wait_recv()
    scale = 0.1 * (slot_ref[c].astype(F32) + 1.0)
    for e in range(2):
        theta = scale * par[e, 0:1, :]
        cosines[e] = jnp.cos(theta)
        sines[e] = jnp.sin(theta)
    oper_wait.wait_recv()
    for p in range(2):
        opt[1 - c, p] = opn[1 - c, p].T
    gacc[...] = jnp.zeros_like(gacc)

    def wait_box(source):
        @pl.when(source != f)
        def _():
            pltpu.make_async_remote_copy(
                src_ref=outbox.at[source],
                dst_ref=inbox.at[source],
                send_sem=box_send.at[source],
                recv_sem=box_recv.at[source],
                device_id={"freq": source},
                device_id_type=MESH,
            ).wait_recv()

    def bin_chunk(j):
        start = SH * j
        first_source = start // SHOTS_DEV
        after = (start + SH - 1) // SHOTS_DEV + 1
        fresh = jnp.where(j == 0, 0, (start - 1) // SHOTS_DEV + 1)

        @pl.loop(fresh, after)
        def _(source):
            wait_box(source)

        row = lax.broadcasted_iota(jnp.int32, (4 * SH, 4 * 128), 0).astype(F32)
        lane_row = lax.broadcasted_iota(jnp.int32, (128, 4 * 128), 0).astype(F32)

        def add_source(source, total):
            tile = inbox[source].astype(F32)
            real, imag = lanes(tile, 0, 512), lanes(tile, 1, 512)
            first, low = lanes(tile, 2, 512), lanes(tile, 3, 512)
            shot = jnp.floor(first * 0.25)
            high = first - 4.0 * shot
            place = shot + (SHOTS_DEV * source - start).astype(F32)
            inside = (place >= 0.0) & (place < float(SH))
            target = jnp.where(inside, high * float(SH) + place, -1.0)
            hit = row == target
            left = jnp.concatenate(
                [jnp.where(hit, real, 0.0).astype(BF16), jnp.where(hit, imag, 0.0).astype(BF16)], axis=0
            )
            right = jnp.where(lane_row == low, 1.0, 0.0).astype(BF16)
            return total + lax.dot_general(left, right, (((1,), (1,)), ((), ())), preferred_element_type=F32)

        total = lax.fori_loop(first_source, after, add_source, jnp.zeros((8 * SH, 128), F32))
        for p in range(2):
            for high in range(4):
                at = (4 * p + high) * SH
                din[j, p, :, 128 * high : 128 * (high + 1)] = total[at : at + SH].astype(BF16)

    def down_copy(j):
        return pltpu.make_async_remote_copy(
            src_ref=dout.at[j],
            dst_ref=din.at[j],
            send_sem=down_send.at[j],
            recv_sem=down_recv.at[j],
            device_id=below,
            device_id_type=MESH,
        )

    def up_copy(j):
        return pltpu.make_async_remote_copy(
            src_ref=abuf.at[0, j],
            dst_ref=uin.at[j],
            send_sem=up_send.at[j],
            recv_sem=up_recv.at[j],
            device_id=above,
            device_id_type=MESH,
        )

    def shift(e, j, real, imag):
        cos_row, sin_row = cosines[e], sines[e]
        shifted_real = (cos_row * real - sin_row * imag).astype(BF16)
        shifted_imag = (cos_row * imag + sin_row * real).astype(BF16)
        vbuf[e, j, 0] = shifted_real
        vbuf[e, j, 1] = shifted_imag
        return jnp.concatenate([shifted_real, shifted_imag], axis=0)

    def forward(e, stacked):
        by_real = product(stacked, opt[e, 0])
        by_imag = product(stacked, opt[e, 1])
        return (by_real[:SH] - by_imag[SH:]).astype(BF16), (by_imag[:SH] + by_real[SH:]).astype(BF16)

    def down(j):
        @pl.when(z == 0)
        def _():
            bin_chunk(j)

        @pl.when(z > 0)
        def _():
            down_copy(j).wait_recv()

        stacked = shift(0, j, din[j, 0].astype(F32), din[j, 1].astype(F32))
        real, imag = forward(0, stacked)
        stacked = shift(1, j, real.astype(F32), imag.astype(F32))

        @pl.when(z < last)
        def _():
            real, imag = forward(1, stacked)
            dout[j, 0] = real
            dout[j, 1] = imag
            down_copy(j).start()

    def tops_here(e, j):
        return pltpu.make_async_copy(
            abuf.at[e, j], tops_ref.at[0, c, :, pl.ds(pl.multiple_of(j * SH, SH), SH), :], tops_local.at[j]
        )

    def tops_there(e, j, slot):
        return pltpu.make_async_remote_copy(
            src_ref=abuf.at[e, j],
            dst_ref=tops_ref.at[0, slot, :, pl.ds(pl.multiple_of(j * SH, SH), SH), :],
            send_sem=tops_send.at[j],
            recv_sem=tops_recv.at[j],
            device_id=partner,
            device_id_type=MESH,
        )

    def backward(e, j, real, imag):
        old_real, old_imag = vbuf[e, j, 0].astype(F32), vbuf[e, j, 1].astype(F32)
        model = par[e, 1:2, :]
        source_real = real + model * old_real
        source_imag = imag + model * old_imag
        term = old_real * source_real + old_imag * source_imag
        gacc[e] += jnp.sum(term.reshape(SH // 8, 8, lateral), axis=0)
        stacked = jnp.concatenate([source_real.astype(BF16), source_imag.astype(BF16)], axis=0)
        by_real = product(stacked, opn[e, 0])
        by_imag = product(stacked, opn[e, 1])
        back_real = by_real[:SH] + by_imag[SH:]
        back_imag = by_real[SH:] - by_imag[:SH]
        cos_row, sin_row = cosines[e], sines[e]
        out_real = (cos_row * back_real + sin_row * back_imag).astype(BF16)
        out_imag = (cos_row * back_imag - sin_row * back_real).astype(BF16)
        abuf[e, j, 0] = out_real
        abuf[e, j, 1] = out_imag

        if e == 0:
            @pl.when(z > 0)
            def _():
                up_copy(j).start()

        @pl.when(c == e)
        def _():
            tops_here(e, j).start()

        @pl.when(c != e)
        def _():
            tops_there(e, j, c).start()

        return out_real, out_imag

    def up(j):
        @pl.when(z < last)
        def _():
            up_copy(j).wait_recv()

        real, imag = backward(1, j, uin[j, 0].astype(F32), uin[j, 1].astype(F32))
        backward(0, j, real.astype(F32), imag.astype(F32))

    @pl.when(z == last)
    def _():
        uin[...] = jnp.zeros_like(uin)

    @pl.loop(0, chunks)
    def _(j):
        down(j)

        @pl.when(z == last)
        def _():
            up(j)

    @pl.when(z < last)
    def _():
        @pl.loop(0, chunks)
        def _(j):
            up(j)

    row8 = lax.broadcasted_iota(jnp.int32, (8, 128), 0)
    tile = jnp.zeros((8, 128), F32)
    for e in range(2):
        summed = jnp.sum(gacc[e], axis=0, keepdims=True)
        for q in range(4):
            tile = jnp.where(row8 == 4 * e + q, summed[:, 128 * q : 128 * (q + 1)], tile)
    gsend[...] = tile

    def g_copy(k):
        return pltpu.make_async_remote_copy(
            src_ref=gsend,
            dst_ref=gbox.at[f],
            send_sem=g_send.at[k],
            recv_sem=g_recv.at[f],
            device_id={"freq": (f + k) % n_freq},
            device_id_type=MESH,
        )

    @pl.loop(1, n_freq)
    def _(k):
        g_copy(k).start()

    gbox[f] = tile

    @pl.loop(1, n_freq)
    def _(k):
        source = (f + k) % n_freq
        pltpu.make_async_remote_copy(
            src_ref=gsend,
            dst_ref=gbox.at[source],
            send_sem=g_send.at[k],
            recv_sem=g_recv.at[source],
            device_id={"freq": source},
            device_id_type=MESH,
        ).wait_recv()

    gpair[0] = jnp.sum(gbox[...], axis=0)
    pair_copy = core_copy(gpair.at[0], gpair.at[1], 2)
    pair_copy.start()
    pair_copy.wait_recv()
    both = gpair[0] + gpair[1]
    mine = jnp.where(c == 0, both[0:4], both[4:8]) * (1.0 / (2.0 * n_freq * SHOTS_DEV * n_freq))
    grad_ref[...] = jnp.concatenate([mine[q : q + 1] for q in range(4)], axis=1)

    pair_copy.wait_send()
    oper_copy.wait_send()
    par_copy.wait_send()

    @pl.loop(1, n_freq)
    def _(k):
        g_copy(k).wait_send()

    @pl.when(z == 0)
    def _():
        @pl.loop(1, n_freq)
        def _(k):
            box_copy(k).wait_send()

    @pl.loop(0, chunks)
    def _(j):
        @pl.when(z < last)
        def _():
            down_copy(j).wait_send()

        @pl.when(z > 0)
        def _():
            up_copy(j).wait_send()

        tops_here(c, j).wait()
        tops_there(1 - c, j, c).wait_send()
        tops_there(1 - c, j, 1 - c).wait_recv()


def body(traces, shot_of_trace, receiver_cell, slot_freq, operators, slowness, image_model):
    n_freq = lax.axis_size("freq")
    n_depth = lax.axis_size("depth")
    local_freqs = operators.shape[1]
    lateral = operators.shape[-1]
    shot_total = SHOTS_DEV * n_freq
    chunks = shot_total // SH
    block = (2, SH, lateral)
    vmem = pl.BlockSpec(memory_space=pltpu.VMEM)
    dma = pltpu.SemaphoreType.DMA
    gradient, tops = pl.pallas_call(
        functools.partial(kernel, n_depth, n_freq),
        out_shape=(
            jax.ShapeDtypeStruct((1, lateral), F32),
            jax.ShapeDtypeStruct((1, local_freqs, 2, shot_total, lateral), BF16),
        ),
        in_specs=[pl.BlockSpec(memory_space=pltpu.SMEM)] + [vmem] * 5 + [pl.BlockSpec(memory_space=pl.ANY)],
        out_specs=(vmem, pl.BlockSpec(memory_space=pl.ANY)),
        scratch_shapes=[
            pltpu.VMEM((2, 2, lateral, lateral), BF16),
            pltpu.VMEM((2, 2, lateral, lateral), BF16),
            pltpu.VMEM((2, 8, lateral), F32),
            pltpu.VMEM((2, 1, lateral), F32),
            pltpu.VMEM((2, 1, lateral), F32),
            pltpu.VMEM((n_freq, 16, 128), BF16),
            pltpu.VMEM((n_freq, 16, 128), BF16),
            pltpu.VMEM((chunks,) + block, BF16),
            pltpu.VMEM((chunks,) + block, BF16),
            pltpu.VMEM((2, chunks) + block, BF16),
            pltpu.VMEM((chunks,) + block, BF16),
            pltpu.VMEM((2, chunks) + block, BF16),
            pltpu.VMEM((2, 8, lateral), F32),
            pltpu.VMEM((8, 128), F32),
            pltpu.VMEM((n_freq, 8, 128), F32),
            pltpu.VMEM((2, 8, 128), F32),
            dma(()),
            dma((3,)),
            dma((3,)),
            dma((n_freq,)),
            dma((n_freq,)),
            dma((chunks,)),
            dma((chunks,)),
            dma((chunks,)),
            dma((chunks,)),
            dma((chunks,)),
            dma((chunks,)),
            dma((chunks,)),
            dma((n_freq,)),
            dma((n_freq,)),
        ],
        compiler_params=pltpu.CompilerParams(
            collective_id=0, has_side_effects=True, vmem_limit_bytes=48 * 2**20
        ),
        cost_estimate=pl.CostEstimate(flops=2 * 10**9, bytes_accessed=4 * 10**6, transcendentals=4096),
        name="migrate",
    )(slot_freq, traces, shot_of_trace, receiver_cell, slowness, image_model, operators)
    return gradient, tops


def solution(mesh):
    in_specs = (
        P("freq", None),
        P("freq", None),
        P("freq", None),
        P("freq"),
        P("depth", "freq", None, None, None),
        P("depth", None),
        P("depth", None),
    )
    out_specs = (P("depth", None), P("depth", "freq", None, None, None))
    return jax.shard_map(body, mesh=mesh, in_specs=in_specs, out_specs=out_specs, check_vma=False)
```

```python
import functools

import jax
import jax.numpy as jnp
from jax import lax
from jax.experimental import pallas as pl
from jax.experimental.pallas import tpu as pltpu
from jax.sharding import PartitionSpec as P

MESH = pl.DeviceIdType.MESH
SHOTS_DEV = 6
SH = 32
SINGLES = 4
F32 = jnp.float32
BF16 = jnp.bfloat16


def product(rows, matrix):
    return jnp.dot(rows, matrix, preferred_element_type=F32)


def product_rows(rows, matrix):
    return lax.dot_general(rows, matrix, (((1,), (1,)), ((), ())), preferred_element_type=F32)


def lanes(tile, row, width):
    return jnp.concatenate([tile[4 * q + row : 4 * q + row + 1] for q in range(width // 128)], axis=1)


def kernel(
    n_depth,
    n_freq,
    slot_hbm,
    traces_hbm,
    shot_hbm,
    cell_hbm,
    slow_hbm,
    model_hbm,
    oper_ref,
    grad_ref,
    tops_ref,
    slot_ref,
    traces_ref,
    shot_ref,
    cell_ref,
    slow_ref,
    model_ref,
    opn,
    opt,
    par,
    cosines,
    sines,
    outbox,
    inbox,
    bins,
    din,
    dout,
    vbuf,
    uin,
    abuf,
    gacc,
    gpart,
    gin,
    gsend,
    gbox,
    load_sem,
    oper_send,
    oper_recv,
    par_send,
    par_recv,
    box_send,
    box_recv,
    down_send,
    down_recv,
    up_send,
    up_recv,
    tops_local,
    tops_send,
    tops_recv,
    part_send,
    part_recv,
    g_send,
    g_recv,
):
    d = lax.axis_index("depth")
    f = lax.axis_index("freq")
    z = d // 2
    c = d % 2
    chunks = din.shape[0]
    lateral = din.shape[-1]
    single = z < SINGLES
    paired = z >= SINGLES
    final = z >= n_depth // 2 - 2
    side = z % 2
    slot = jnp.where(single, c, side)
    rank = jnp.where(single, c, 2 * side + c)
    base = d - rank
    mine = jnp.where(single, chunks, chunks // 2)
    partner = base + jnp.where(single, 1 - c, 2 * side + 1 - c)
    across = base + 2 * (1 - side) + c
    across_other = base + 2 * (1 - side) + 1 - c
    edge = 2 * SINGLES

    def at(depth):
        return {"depth": depth}

    def place_of(turn):
        return jnp.where(single, turn, 2 * turn + c)

    first_chunk = (f * SHOTS_DEV) // SH

    def chunk_of(place):
        return (first_chunk + place) % chunks

    def down_target(place):
        return jnp.where(z < SINGLES - 1, d + 2, jnp.where(single, edge + 2 * c + place % 2, (d + 4) % n_depth))

    up_target = jnp.where(single, (d + n_depth - 2) % n_depth, jnp.where(z < SINGLES + 2, edge - 2 + side, d - 4))

    barrier = pltpu.get_barrier_semaphore()

    def greet(depth):
        pl.semaphore_signal(barrier, inc=1, device_id=at(depth), device_id_type=MESH)

    @pl.loop(1, n_freq)
    def _(k):
        pl.semaphore_signal(barrier, inc=1, device_id={"freq": (f + k) % n_freq}, device_id_type=MESH)

    greet(partner)

    @pl.when(z > 0)
    def _():
        greet(up_target)

    @pl.when(jnp.logical_not(final))
    def _():
        greet(down_target(0))

    @pl.when(z == SINGLES - 1)
    def _():
        greet(down_target(1))

    @pl.when(paired)
    def _():
        greet(across)
        greet(across_other)

    greeted = (
        n_freq
        + jnp.where(z > 0, 1, 0)
        + jnp.where(final, 0, 1)
        + jnp.where(z == SINGLES - 1, 1, 0)
        + jnp.where(paired, 2, 0)
    )

    loads = [
        pltpu.make_async_copy(source, target, load_sem.at[i])
        for i, (source, target) in enumerate(
            [
                (slow_hbm, slow_ref),
                (model_hbm, model_ref),
                (slot_hbm, slot_ref),
                (traces_hbm, traces_ref),
                (shot_hbm, shot_ref),
                (cell_hbm, cell_ref),
                (oper_ref.at[0, slot], opn.at[rank]),
            ]
        )
    ]

    @pl.when(z == 0)
    def _():
        for load in loads[3:6]:
            load.start()

    for load in loads[:3] + loads[6:]:
        load.start()
    for load in loads[:2]:
        load.wait()

    row8 = lax.broadcasted_iota(jnp.int32, (8, lateral), 0)
    par[rank] = jnp.where(row8 == 0, slow_ref[...], model_ref[...])

    @pl.when(z == 0)
    def _():
        for load in loads[3:6]:
            load.wait()
        rows = n_freq * 16
        row = lax.broadcasted_iota(jnp.int32, (rows, 128), 0)
        column = lax.broadcasted_iota(jnp.int32, (rows, 128), 1)
        group, within = row // 16, row % 16
        kind, piece = within % 4, within // 4
        wanted = jnp.where(kind < 2, group * 4 + 2 * c + kind, -1)
        total = jnp.zeros((rows, 128), F32)
        for q in range(4):
            select = jnp.where((column == wanted) & (piece == q), 1.0, 0.0).astype(BF16)
            total += lax.dot_general(
                select,
                traces_ref[128 * q : 128 * (q + 1), :],
                (((1,), (1,)), ((), ())),
                preferred_element_type=F32,
            )
        cell = cell_ref[...]
        first = (cell // 128 * 8 + shot_ref[...]).astype(F32)
        second = (cell % 128).astype(F32)
        row16 = lax.broadcasted_iota(jnp.int32, (16, 128), 0)
        label = jnp.zeros((16, 128), F32)
        for q in range(4):
            label = jnp.where(row16 == 4 * q + 2, first[:, 128 * q : 128 * (q + 1)], label)
            label = jnp.where(row16 == 4 * q + 3, second[:, 128 * q : 128 * (q + 1)], label)
        filled = total.reshape(n_freq, 16, 128) + label[None]
        outbox[...] = filled.astype(BF16)
        inbox[f] = outbox[f]

    pl.semaphore_wait(barrier, greeted)

    def box_copy(k):
        return pltpu.make_async_remote_copy(
            src_ref=outbox.at[(f + k) % n_freq],
            dst_ref=inbox.at[f],
            send_sem=box_send.at[k],
            recv_sem=box_recv.at[f],
            device_id={"freq": (f + k) % n_freq},
            device_id_type=MESH,
        )

    @pl.when(z == 0)
    def _():
        @pl.loop(1, n_freq // 2)
        def _(k):
            box_copy(k).start()
            box_copy(n_freq - k).start()

        box_copy(n_freq // 2).start()

    def par_copy(mate, index, target):
        return pltpu.make_async_remote_copy(
            src_ref=par.at[index],
            dst_ref=par.at[index],
            send_sem=par_send.at[mate],
            recv_sem=par_recv.at[index],
            device_id=at(target),
            device_id_type=MESH,
        )

    def oper_copy(source, index, send, target):
        return pltpu.make_async_remote_copy(
            src_ref=source,
            dst_ref=opn.at[index],
            send_sem=oper_send.at[send],
            recv_sem=oper_recv.at[index, 0],
            device_id=at(target),
            device_id_type=MESH,
        )

    def half_copy(source, index, p, send, target):
        return pltpu.make_async_remote_copy(
            src_ref=source,
            dst_ref=opn.at[index, p],
            send_sem=oper_send.at[send],
            recv_sem=oper_recv.at[index, p],
            device_id=at(target),
            device_id_type=MESH,
        )

    partner_rank = partner - base
    across_rank = across - base
    other_rank = across_other - base
    to_partner = oper_copy(oper_ref.at[0, jnp.where(single, 1 - c, side)], rank, 0, partner)
    from_partner = oper_copy(oper_ref.at[0, slot], partner_rank, 0, partner)

    @pl.when(paired)
    def _():
        for p in range(2):
            half_copy(oper_ref.at[0, 1 - side, p], rank, p, 1 + p, across).start()

    par_copy(0, rank, partner).start()
    to_partner.start()

    @pl.when(paired)
    def _():
        par_copy(1, rank, across).start()
        par_copy(2, rank, across_other).start()

    loads[2].wait()
    loads[6].wait()
    scale = 0.1 * (slot_ref[slot].astype(F32) + 1.0)

    def angles(e):
        theta = scale * par[e, 0:1, :]
        cosines[e] = jnp.cos(theta)
        sines[e] = jnp.sin(theta)

    gacc[...] = jnp.zeros_like(gacc)

    @pl.when(single)
    def _():
        for p in range(2):
            opt[rank, p] = opn[rank, p].T

    par_copy(0, partner_rank, partner).wait_recv()
    angles(rank)
    angles(partner_rank)
    from_partner.wait_recv()

    @pl.when(single)
    def _():
        for p in range(2):
            opt[partner_rank, p] = opn[partner_rank, p].T

    @pl.when(paired)
    def _():
        par_copy(1, across_rank, across).wait_recv()
        par_copy(2, other_rank, across_other).wait_recv()
        angles(across_rank)
        angles(other_rank)
        for p in range(2):
            half_copy(oper_ref.at[0, slot, p], across_rank, p, 1 + p, across).wait_recv()
            half_copy(opn.at[across_rank, p], across_rank, p, 3 + p, partner).start()
        for p in range(2):
            half_copy(opn.at[other_rank, p], other_rank, p, 3 + p, partner).wait_recv()

    def wait_box(source):
        @pl.when(source != f)
        def _():
            pltpu.make_async_remote_copy(
                src_ref=outbox.at[source],
                dst_ref=inbox.at[source],
                send_sem=box_send.at[source],
                recv_sem=box_recv.at[source],
                device_id={"freq": source},
                device_id_type=MESH,
            ).wait_recv()

    sources = max((SH * j + SH - 1) // SHOTS_DEV - SH * j // SHOTS_DEV + 1 for j in range(chunks))

    def bin_chunk(place):
        j = chunk_of(place)
        start = SH * j
        first_source = start // SHOTS_DEV
        fresh = jnp.where(place == 0, first_source, (start + SHOTS_DEV - 1) // SHOTS_DEV)
        after = jnp.where(
            (place == chunks - 1) & (first_chunk > 0),
            (SH * first_chunk) // SHOTS_DEV,
            (start + SH - 1) // SHOTS_DEV + 1,
        )

        @pl.loop(fresh, after)
        def _(source):
            wait_box(source)

        top = 8 + SHOTS_DEV * first_source - start
        row = lax.broadcasted_iota(jnp.int32, (32, 4 * 128), 0).astype(F32)
        lane_row = lax.broadcasted_iota(jnp.int32, (128, 4 * 128), 0).astype(F32)
        for i in range(sources):
            tile = inbox[first_source + i].astype(F32)
            real, imag = lanes(tile, 0, 512), lanes(tile, 1, 512)
            first, low = lanes(tile, 2, 512), lanes(tile, 3, 512)
            hit = row == first
            left = jnp.concatenate(
                [jnp.where(hit, real, 0.0).astype(BF16), jnp.where(hit, imag, 0.0).astype(BF16)], axis=0
            )
            right = jnp.where(lane_row == low, 1.0, 0.0).astype(BF16)
            part = lax.dot_general(left, right, (((1,), (1,)), ((), ())), preferred_element_type=F32)
            for g in range(8):
                bins[g, pl.ds(top + SHOTS_DEV * i, 8), :] = part[8 * g : 8 * (g + 1)]
        for p in range(2):
            for high in range(4):
                din[place, p, :, 128 * high : 128 * (high + 1)] = bins[4 * p + high, 8 : 8 + SH, :].astype(BF16)

    def down_copy(place):
        return pltpu.make_async_remote_copy(
            src_ref=dout.at[place],
            dst_ref=din.at[place],
            send_sem=down_send.at[place],
            recv_sem=down_recv.at[place],
            device_id=at(down_target(place)),
            device_id_type=MESH,
        )

    def up_copy(place):
        return pltpu.make_async_remote_copy(
            src_ref=abuf.at[0, place],
            dst_ref=uin.at[place],
            send_sem=up_send.at[place],
            recv_sem=up_recv.at[place],
            device_id=at(up_target),
            device_id_type=MESH,
        )

    def shift(e, place, real, imag):
        cos_row, sin_row = cosines[e], sines[e]
        shifted_real = (cos_row * real - sin_row * imag).astype(BF16)
        shifted_imag = (cos_row * imag + sin_row * real).astype(BF16)
        vbuf[e, place, 0] = shifted_real
        vbuf[e, place, 1] = shifted_imag
        return jnp.concatenate([shifted_real, shifted_imag], axis=0)

    def forward(stacked, by_real, by_imag):
        return (by_real[:SH] - by_imag[SH:]).astype(BF16), (by_imag[:SH] + by_real[SH:]).astype(BF16)

    def forward_single(e, stacked):
        return forward(stacked, product(stacked, opt[e, 0]), product(stacked, opt[e, 1]))

    def forward_pair(e, stacked):
        return forward(stacked, product_rows(stacked, opn[e, 0]), product_rows(stacked, opn[e, 1]))

    def send_down(place, real, imag):
        dout[place, 0] = real
        dout[place, 1] = imag
        down_copy(place).start()

    def down_single(place):
        stacked = shift(0, place, din[place, 0].astype(F32), din[place, 1].astype(F32))
        real, imag = forward_single(0, stacked)
        stacked = shift(1, place, real.astype(F32), imag.astype(F32))
        real, imag = forward_single(1, stacked)
        send_down(place, real, imag)

    def down_pair(place):
        real, imag = din[place, 0], din[place, 1]
        for e in range(3):
            stacked = shift(e, place, real.astype(F32), imag.astype(F32))
            real, imag = forward_pair(e, stacked)
        stacked = shift(3, place, real.astype(F32), imag.astype(F32))

        @pl.when(jnp.logical_not(final))
        def _():
            real, imag = forward_pair(3, stacked)
            send_down(place, real, imag)

    def rows_of(place):
        return pl.ds(pl.multiple_of(chunk_of(place) * SH, SH), SH)

    def tops_here(e, place):
        return pltpu.make_async_copy(abuf.at[e, place], tops_ref.at[0, slot, :, rows_of(place), :], tops_local.at[place])

    def tops_there(e, place, its_slot):
        return pltpu.make_async_remote_copy(
            src_ref=abuf.at[e, place],
            dst_ref=tops_ref.at[0, its_slot, :, rows_of(place), :],
            send_sem=tops_send.at[e, place],
            recv_sem=tops_recv.at[its_slot, place],
            device_id=at(base + e),
            device_id_type=MESH,
        )

    def backward(e, place, real, imag):
        old_real, old_imag = vbuf[e, place, 0].astype(F32), vbuf[e, place, 1].astype(F32)
        model = par[e, 1:2, :]
        source_real = real + model * old_real
        source_imag = imag + model * old_imag
        term = old_real * source_real + old_imag * source_imag
        gacc[e] += jnp.sum(term.reshape(SH // 8, 8, lateral), axis=0)
        stacked = jnp.concatenate([source_real.astype(BF16), source_imag.astype(BF16)], axis=0)
        by_real = product(stacked, opn[e, 0])
        by_imag = product(stacked, opn[e, 1])
        back_real = by_real[:SH] + by_imag[SH:]
        back_imag = by_real[SH:] - by_imag[:SH]
        cos_row, sin_row = cosines[e], sines[e]
        out_real = (cos_row * back_real + sin_row * back_imag).astype(BF16)
        out_imag = (cos_row * back_imag - sin_row * back_real).astype(BF16)
        abuf[e, place, 0] = out_real
        abuf[e, place, 1] = out_imag

        if e == 0:

            @pl.when(z > 0)
            def _():
                up_copy(place).start()

        @pl.when(rank == e)
        def _():
            tops_here(e, place).start()

        @pl.when(rank != e)
        def _():
            tops_there(e, place, slot).start()

        return out_real.astype(F32), out_imag.astype(F32)

    def up(place, steps):
        real, imag = uin[place, 0].astype(F32), uin[place, 1].astype(F32)
        for e in reversed(range(steps)):
            real, imag = backward(e, place, real, imag)

    @pl.when(single)
    def _():
        @pl.loop(0, chunks)
        def _(place):
            @pl.when(z == 0)
            def _():
                bin_chunk(place)

            @pl.when(z > 0)
            def _():
                down_copy(place).wait_recv()

            down_single(place)

        @pl.loop(0, chunks)
        def _(place):
            up_copy(place).wait_recv()
            up(place, 2)

    @pl.when(final)
    def _():
        uin[...] = jnp.zeros_like(uin)

    @pl.when(paired)
    def _():
        @pl.loop(0, 2 * mine)
        def _(turn):
            going_down = jnp.where(final, turn % 2 == 0, turn < mine)
            place = place_of(jnp.where(final, turn // 2, turn % mine))

            @pl.when(going_down)
            def _():
                down_copy(place).wait_recv()
                down_pair(place)

            @pl.when(jnp.logical_not(going_down))
            def _():
                @pl.when(jnp.logical_not(final))
                def _():
                    up_copy(place).wait_recv()

                up(place, 4)

    row4 = lax.broadcasted_iota(jnp.int32, (4, 128), 0)

    def rows_tile(summed):
        tile = jnp.zeros((4, 128), F32)
        for q in range(4):
            tile = jnp.where(row4 == q, summed[:, 128 * q : 128 * (q + 1)], tile)
        return tile

    def part_copy(e, sender):
        return pltpu.make_async_remote_copy(
            src_ref=gpart.at[e],
            dst_ref=gin.at[sender],
            send_sem=part_send.at[e],
            recv_sem=part_recv.at[sender],
            device_id=at(base + e),
            device_id_type=MESH,
        )

    def share(steps):
        for e in range(steps):
            gpart[e] = rows_tile(jnp.sum(gacc[e], axis=0, keepdims=True))

            @pl.when(rank != e)
            def _():
                part_copy(e, rank).start()

        total = gpart[rank]
        for e in range(steps):

            @pl.when(rank != e)
            def _():
                part_copy(e, e).wait_recv()

            @pl.when(rank == e)
            def _():
                gin[e] = jnp.zeros((4, 128), F32)

        for e in range(steps):
            total = total + gin[e]
        gsend[...] = total
        gbox[f] = total

    @pl.when(single)
    def _():
        share(2)

    @pl.when(paired)
    def _():
        share(4)

    def g_copy(k):
        return pltpu.make_async_remote_copy(
            src_ref=gsend,
            dst_ref=gbox.at[f],
            send_sem=g_send.at[k],
            recv_sem=g_recv.at[f],
            device_id={"freq": (f + k) % n_freq},
            device_id_type=MESH,
        )

    @pl.loop(1, n_freq)
    def _(k):
        g_copy(k).start()

    @pl.loop(1, n_freq)
    def _(k):
        source = (f + k) % n_freq
        pltpu.make_async_remote_copy(
            src_ref=gsend,
            dst_ref=gbox.at[source],
            send_sem=g_send.at[k],
            recv_sem=g_recv.at[source],
            device_id={"freq": source},
            device_id_type=MESH,
        ).wait_recv()

    total = jnp.sum(gbox[...], axis=0) * (1.0 / (2.0 * n_freq * SHOTS_DEV * n_freq))
    grad_ref[...] = jnp.concatenate([total[q : q + 1] for q in range(4)], axis=1)

    to_partner.wait_send()
    par_copy(0, rank, partner).wait_send()

    @pl.when(paired)
    def _():
        par_copy(1, rank, across).wait_send()
        par_copy(2, rank, across_other).wait_send()
        for p in range(2):
            half_copy(oper_ref.at[0, 1 - side, p], rank, p, 1 + p, across).wait_send()
            half_copy(opn.at[across_rank, p], across_rank, p, 3 + p, partner).wait_send()

    @pl.loop(1, n_freq)
    def _(k):
        g_copy(k).wait_send()

    @pl.when(z == 0)
    def _():
        @pl.loop(1, n_freq)
        def _(k):
            box_copy(k).wait_send()

    steps = jnp.where(single, 2, 4)

    @pl.loop(0, steps)
    def _(e):
        @pl.when(rank != e)
        def _():
            part_copy(e, rank).wait_send()

            @pl.loop(0, mine)
            def _(turn):
                tops_there(e, place_of(turn), slot).wait_send()

    @pl.loop(0, mine)
    def _(turn):
        place = place_of(turn)

        @pl.when(jnp.logical_not(final))
        def _():
            down_copy(place).wait_send()

        @pl.when(z > 0)
        def _():
            up_copy(place).wait_send()

        tops_here(rank, place).wait()

    @pl.loop(0, 2 * chunks)
    def _(index):
        its_slot, place = index // chunks, index % chunks
        sender = jnp.where(single, its_slot, 2 * its_slot + place % 2)

        @pl.when(sender != rank)
        def _():
            tops_there(rank, place, its_slot).wait_recv()


def body(traces, shot_of_trace, receiver_cell, slot_freq, operators, slowness, image_model):
    n_freq = lax.axis_size("freq")
    n_depth = lax.axis_size("depth")
    local_freqs = operators.shape[1]
    lateral = operators.shape[-1]
    shot_total = SHOTS_DEV * n_freq
    chunks = shot_total // SH
    block = (2, SH, lateral)
    vmem = pl.BlockSpec(memory_space=pltpu.VMEM)
    dma = pltpu.SemaphoreType.DMA
    gradient, tops = pl.pallas_call(
        functools.partial(kernel, n_depth, n_freq),
        out_shape=(
            jax.ShapeDtypeStruct((1, lateral), F32),
            jax.ShapeDtypeStruct((1, local_freqs, 2, shot_total, lateral), BF16),
        ),
        in_specs=[pl.BlockSpec(memory_space=pltpu.HBM)] * 7,
        out_specs=(vmem, pl.BlockSpec(memory_space=pl.ANY)),
        scratch_shapes=[
            pltpu.SMEM(slot_freq.shape, jnp.int32),
            pltpu.VMEM(traces.shape, BF16),
            pltpu.VMEM(shot_of_trace.shape, jnp.int32),
            pltpu.VMEM(receiver_cell.shape, jnp.int32),
            pltpu.VMEM(slowness.shape, F32),
            pltpu.VMEM(image_model.shape, F32),
            pltpu.VMEM((4, 2, lateral, lateral), BF16),
            pltpu.VMEM((2, 2, lateral, lateral), BF16),
            pltpu.VMEM((4, 8, lateral), F32),
            pltpu.VMEM((4, 1, lateral), F32),
            pltpu.VMEM((4, 1, lateral), F32),
            pltpu.VMEM((n_freq, 16, 128), BF16),
            pltpu.VMEM((n_freq, 16, 128), BF16),
            pltpu.VMEM((8, SH + 32, 128), F32),
            pltpu.VMEM((chunks,) + block, BF16),
            pltpu.VMEM((chunks,) + block, BF16),
            pltpu.VMEM((4, chunks) + block, BF16),
            pltpu.VMEM((chunks,) + block, BF16),
            pltpu.VMEM((4, chunks) + block, BF16),
            pltpu.VMEM((4, 8, lateral), F32),
            pltpu.VMEM((4, 4, 128), F32),
            pltpu.VMEM((4, 4, 128), F32),
            pltpu.VMEM((4, 128), F32),
            pltpu.VMEM((n_freq, 4, 128), F32),
            dma((7,)),
            dma((5,)),
            dma((4, 2)),
            dma((3,)),
            dma((4,)),
            dma((n_freq,)),
            dma((n_freq,)),
            dma((chunks,)),
            dma((chunks,)),
            dma((chunks,)),
            dma((chunks,)),
            dma((chunks,)),
            dma((4, chunks)),
            dma((2, chunks)),
            dma((4,)),
            dma((4,)),
            dma((n_freq,)),
            dma((n_freq,)),
        ],
        compiler_params=pltpu.CompilerParams(
            collective_id=0, has_side_effects=True, vmem_limit_bytes=60 * 2**20
        ),
        cost_estimate=pl.CostEstimate(flops=2 * 10**9, bytes_accessed=4 * 10**6, transcendentals=4096),
        name="migrate",
    )(slot_freq, traces, shot_of_trace, receiver_cell, slowness, image_model, operators)
    return gradient, tops


def solution(mesh):
    in_specs = (
        P("freq", None),
        P("freq", None),
        P("freq", None),
        P("freq"),
        P("depth", "freq", None, None, None),
        P("depth", None),
        P("depth", None),
    )
    out_specs = (P("depth", None), P("depth", "freq", None, None, None))
    return jax.shard_map(body, mesh=mesh, in_specs=in_specs, out_specs=out_specs, check_vma=False)
```

```python
import functools

import jax
import jax.numpy as jnp
from jax import lax
from jax.experimental import pallas as pl
from jax.experimental.pallas import tpu as pltpu
from jax.sharding import PartitionSpec as P

MESH = pl.DeviceIdType.MESH
SHOTS_DEV = 6
SH = 32
HALF = 2
F32 = jnp.float32
BF16 = jnp.bfloat16


def product(rows, matrix):
    return jnp.dot(rows, matrix, preferred_element_type=F32)


def product_rows(rows, matrix):
    return lax.dot_general(rows, matrix, (((1,), (1,)), ((), ())), preferred_element_type=F32)


def lanes(tile, row, width):
    return jnp.concatenate([tile[4 * q + row : 4 * q + row + 1] for q in range(width // 128)], axis=1)


def kernel(
    n_depth,
    n_freq,
    slot_hbm,
    traces_hbm,
    shot_hbm,
    cell_hbm,
    slow_hbm,
    model_hbm,
    oper_ref,
    grad_ref,
    tops_ref,
    slot_ref,
    traces_ref,
    shot_ref,
    cell_ref,
    slow_ref,
    model_ref,
    opn,
    opt,
    par,
    cosines,
    sines,
    outbox,
    inbox,
    bins,
    din,
    dout,
    vbuf,
    uin,
    abuf,
    gacc,
    gpart,
    gin,
    gsend,
    gbox,
    load_sem,
    oper_send,
    oper_recv,
    par_send,
    par_recv,
    box_send,
    box_recv,
    down_send,
    down_recv,
    up_send,
    up_recv,
    tops_local,
    tops_send,
    tops_recv,
    part_send,
    part_recv,
    g_send,
    g_recv,
):
    d = lax.axis_index("depth")
    f = lax.axis_index("freq")
    z = d // 2
    c = d % 2
    chunks = din.shape[0]
    lateral = din.shape[-1]
    last = n_depth // 2 - 1
    odd = z % 2 == 1
    host = odd & (z < last)
    helper = jnp.logical_not(odd) & (z > 0)
    base = 2 * z
    partner = base + 1 - c
    cross = jnp.where(host, d + 2, d - 2) + 1 - 2 * c

    def at(depth):
        return {"depth": depth}

    first_chunk = (f * SHOTS_DEV) // SH

    def chunk_of(place):
        return (first_chunk + place) % chunks

    below = (d + 2) % n_depth
    above = (d + n_depth - 2) % n_depth
    up_target = jnp.where(z > 1, (d + n_depth - 4) % n_depth, above)

    barrier = pltpu.get_barrier_semaphore()

    def greet(depth):
        pl.semaphore_signal(barrier, inc=1, device_id=at(depth), device_id_type=MESH)

    @pl.loop(1, n_freq)
    def _(k):
        pl.semaphore_signal(barrier, inc=1, device_id={"freq": (f + k) % n_freq}, device_id_type=MESH)

    greet(partner)

    @pl.when(z > 0)
    def _():
        greet(above)

    @pl.when(z < last)
    def _():
        greet(below)

    @pl.when(host)
    def _():
        greet((d + 4) % n_depth)

    @pl.when(odd & (z > 1))
    def _():
        greet(up_target)

    @pl.when(host | helper)
    def _():
        greet(cross)

    greeted = (
        n_freq
        + jnp.where(z > 0, 1, 0)
        + jnp.where(z < last, 1, 0)
        + jnp.where(host, 1, 0)
        + jnp.where(odd & (z > 1), 1, 0)
        + jnp.where(host | helper, 1, 0)
    )

    loads = [
        pltpu.make_async_copy(source, target, load_sem.at[i])
        for i, (source, target) in enumerate(
            [
                (slow_hbm, slow_ref),
                (model_hbm, model_ref),
                (slot_hbm, slot_ref),
                (traces_hbm, traces_ref),
                (shot_hbm, shot_ref),
                (cell_hbm, cell_ref),
                (oper_ref.at[0, c], opn.at[c]),
            ]
        )
    ]

    @pl.when(z == 0)
    def _():
        for load in loads[3:6]:
            load.start()

    for load in loads[:3] + loads[6:]:
        load.start()
    for load in loads[:2]:
        load.wait()

    row8 = lax.broadcasted_iota(jnp.int32, (8, lateral), 0)
    par[c] = jnp.where(row8 == 0, slow_ref[...], model_ref[...])

    @pl.when(z == 0)
    def _():
        for load in loads[3:6]:
            load.wait()
        rows = n_freq * 16
        row = lax.broadcasted_iota(jnp.int32, (rows, 128), 0)
        column = lax.broadcasted_iota(jnp.int32, (rows, 128), 1)
        group, within = row // 16, row % 16
        kind, piece = within % 4, within // 4
        wanted = jnp.where(kind < 2, group * 4 + 2 * c + kind, -1)
        total = jnp.zeros((rows, 128), F32)
        for q in range(4):
            select = jnp.where((column == wanted) & (piece == q), 1.0, 0.0).astype(BF16)
            total += lax.dot_general(
                select,
                traces_ref[128 * q : 128 * (q + 1), :],
                (((1,), (1,)), ((), ())),
                preferred_element_type=F32,
            )
        cell = cell_ref[...]
        first = (cell // 128 * 8 + shot_ref[...]).astype(F32)
        second = (cell % 128).astype(F32)
        row16 = lax.broadcasted_iota(jnp.int32, (16, 128), 0)
        label = jnp.zeros((16, 128), F32)
        for q in range(4):
            label = jnp.where(row16 == 4 * q + 2, first[:, 128 * q : 128 * (q + 1)], label)
            label = jnp.where(row16 == 4 * q + 3, second[:, 128 * q : 128 * (q + 1)], label)
        filled = total.reshape(n_freq, 16, 128) + label[None]
        outbox[...] = filled.astype(BF16)
        inbox[f] = outbox[f]

    pl.semaphore_wait(barrier, greeted)

    def box_copy(k):
        return pltpu.make_async_remote_copy(
            src_ref=outbox.at[(f + k) % n_freq],
            dst_ref=inbox.at[f],
            send_sem=box_send.at[k],
            recv_sem=box_recv.at[f],
            device_id={"freq": (f + k) % n_freq},
            device_id_type=MESH,
        )

    @pl.when(z == 0)
    def _():
        @pl.loop(1, n_freq // 2)
        def _(k):
            box_copy(k).start()
            box_copy(n_freq - k).start()

        box_copy(n_freq // 2).start()

    def par_copy(index, place, send, target):
        return pltpu.make_async_remote_copy(
            src_ref=par.at[index],
            dst_ref=par.at[place],
            send_sem=par_send.at[send],
            recv_sem=par_recv.at[place],
            device_id=at(target),
            device_id_type=MESH,
        )

    def oper_copy(source, place, target):
        return pltpu.make_async_remote_copy(
            src_ref=source,
            dst_ref=opn.at[place],
            send_sem=oper_send.at[place],
            recv_sem=oper_recv.at[place],
            device_id=at(target),
            device_id_type=MESH,
        )

    to_partner = oper_copy(oper_ref.at[0, 1 - c], c, partner)
    to_partner.start()
    par_copy(c, c, 0, partner).start()

    @pl.when(helper)
    def _():
        par_copy(c, 2 + c, 1, above).start()
        par_copy(c, 2 + c, 2, cross).start()

    def lend(e):
        return oper_copy(opn.at[e], 2 + e, above)

    loads[2].wait()
    loads[6].wait()
    scale = 0.1 * (slot_ref[c].astype(F32) + 1.0)

    def angles(e):
        theta = scale * par[e, 0:1, :]
        cosines[e] = jnp.cos(theta)
        sines[e] = jnp.sin(theta)

    @pl.when(helper & (z > 2))
    def _():
        lend(c).start()

    gacc[...] = jnp.zeros_like(gacc)
    for p in range(2):
        opt[c, p] = opn[c, p].T
    par_copy(1 - c, 1 - c, 0, partner).wait_recv()
    angles(0)
    angles(1)
    oper_copy(oper_ref.at[0, c], 1 - c, partner).wait_recv()

    @pl.when(helper & (z > 2))
    def _():
        lend(1 - c).start()

    for p in range(2):
        opt[1 - c, p] = opn[1 - c, p].T

    def wait_box(source):
        @pl.when(source != f)
        def _():
            pltpu.make_async_remote_copy(
                src_ref=outbox.at[source],
                dst_ref=inbox.at[source],
                send_sem=box_send.at[source],
                recv_sem=box_recv.at[source],
                device_id={"freq": source},
                device_id_type=MESH,
            ).wait_recv()

    sources = max((SH * j + SH - 1) // SHOTS_DEV - SH * j // SHOTS_DEV + 1 for j in range(chunks))

    def bin_chunk(place):
        j = chunk_of(place)
        start = SH * j
        first_source = start // SHOTS_DEV
        fresh = jnp.where(place == 0, first_source, (start + SHOTS_DEV - 1) // SHOTS_DEV)
        after = jnp.where(
            (place == chunks - 1) & (first_chunk > 0),
            (SH * first_chunk) // SHOTS_DEV,
            (start + SH - 1) // SHOTS_DEV + 1,
        )

        @pl.loop(fresh, after)
        def _(source):
            wait_box(source)

        top = 8 + SHOTS_DEV * first_source - start
        row = lax.broadcasted_iota(jnp.int32, (32, 4 * 128), 0).astype(F32)
        lane_row = lax.broadcasted_iota(jnp.int32, (128, 4 * 128), 0).astype(F32)
        for i in range(sources):
            tile = inbox[first_source + i].astype(F32)
            real, imag = lanes(tile, 0, 512), lanes(tile, 1, 512)
            first, low = lanes(tile, 2, 512), lanes(tile, 3, 512)
            hit = row == first
            left = jnp.concatenate(
                [jnp.where(hit, real, 0.0).astype(BF16), jnp.where(hit, imag, 0.0).astype(BF16)], axis=0
            )
            right = jnp.where(lane_row == low, 1.0, 0.0).astype(BF16)
            part = lax.dot_general(left, right, (((1,), (1,)), ((), ())), preferred_element_type=F32)
            for g in range(8):
                bins[g, pl.ds(top + SHOTS_DEV * i, 8), :] = part[8 * g : 8 * (g + 1)]
        for p in range(2):
            for high in range(4):
                din[place, p, :, 128 * high : 128 * (high + 1)] = bins[4 * p + high, 8 : 8 + SH, :].astype(BF16)

    def columns(half):
        width = lateral // HALF
        return pl.ds(half * width, width)

    def down_copy(place, half):
        return pltpu.make_async_remote_copy(
            src_ref=dout.at[place, :, :, columns(half)],
            dst_ref=din.at[place, :, :, columns(half)],
            send_sem=down_send.at[place, half],
            recv_sem=down_recv.at[place, half],
            device_id=at(below),
            device_id_type=MESH,
        )

    def up_copy(place, half):
        return pltpu.make_async_remote_copy(
            src_ref=abuf.at[0, place, :, :, columns(half)],
            dst_ref=uin.at[place, :, :, columns(half)],
            send_sem=up_send.at[place, half],
            recv_sem=up_recv.at[place, half],
            device_id=at(up_target),
            device_id_type=MESH,
        )

    def shift(e, place, real, imag):
        cos_row, sin_row = cosines[e], sines[e]
        shifted_real = (cos_row * real - sin_row * imag).astype(BF16)
        shifted_imag = (cos_row * imag + sin_row * real).astype(BF16)
        vbuf[e, place, 0] = shifted_real
        vbuf[e, place, 1] = shifted_imag
        return jnp.concatenate([shifted_real, shifted_imag], axis=0)

    def forward(stacked, by_real, by_imag):
        return (by_real[:SH] - by_imag[SH:]).astype(BF16), (by_imag[:SH] + by_real[SH:]).astype(BF16)

    def down(place):
        stacked = shift(0, place, din[place, 0].astype(F32), din[place, 1].astype(F32))
        real, imag = forward(stacked, product(stacked, opt[0, 0]), product(stacked, opt[0, 1]))
        stacked = shift(1, place, real.astype(F32), imag.astype(F32))

        @pl.when(z < last)
        def _():
            for half in range(HALF):
                cols = columns(half)
                real, imag = forward(
                    stacked, product(stacked, opt[1, 0, :, cols]), product(stacked, opt[1, 1, :, cols])
                )
                dout[place, 0, :, cols] = real
                dout[place, 1, :, cols] = imag
                down_copy(place, half).start()

    def again(place):
        stacked = shift(2, place, dout[place, 0].astype(F32), dout[place, 1].astype(F32))
        real, imag = forward(stacked, product_rows(stacked, opn[2, 0]), product_rows(stacked, opn[2, 1]))
        shift(3, place, real.astype(F32), imag.astype(F32))

    def rows_of(place):
        return pl.ds(pl.multiple_of(chunk_of(place) * SH, SH), SH)

    def tops_here(e, place):
        return pltpu.make_async_copy(abuf.at[e, place], tops_ref.at[0, c, :, rows_of(place), :], tops_local.at[place])

    def tops_there(e, place, its_slot):
        return pltpu.make_async_remote_copy(
            src_ref=abuf.at[e, place],
            dst_ref=tops_ref.at[0, its_slot, :, rows_of(place), :],
            send_sem=tops_send.at[e, place],
            recv_sem=tops_recv.at[its_slot, place],
            device_id=at(base + e),
            device_id_type=MESH,
        )

    def backward(e, place, real, imag):
        old_real, old_imag = vbuf[e, place, 0].astype(F32), vbuf[e, place, 1].astype(F32)
        model = par[e, 1:2, :]
        source_real = real + model * old_real
        source_imag = imag + model * old_imag
        term = old_real * source_real + old_imag * source_imag
        gacc[e] += jnp.sum(term.reshape(SH // 8, 8, lateral), axis=0)
        stacked = jnp.concatenate([source_real.astype(BF16), source_imag.astype(BF16)], axis=0)
        pieces = HALF if e == 0 else 1
        width = lateral // pieces
        result = []
        for piece in range(pieces):
            cols = pl.ds(piece * width, width)
            by_real = product(stacked, opn[e, 0, :, cols])
            by_imag = product(stacked, opn[e, 1, :, cols])
            back_real = by_real[:SH] + by_imag[SH:]
            back_imag = by_real[SH:] - by_imag[:SH]
            cos_row, sin_row = cosines[e, :, cols], sines[e, :, cols]
            out_real = (cos_row * back_real + sin_row * back_imag).astype(BF16)
            out_imag = (cos_row * back_imag - sin_row * back_real).astype(BF16)
            abuf[e, place, 0, :, cols] = out_real
            abuf[e, place, 1, :, cols] = out_imag
            result = out_real.astype(F32), out_imag.astype(F32)
            if e == 0:

                @pl.when(z > 0)
                def _():
                    up_copy(place, piece).start()

        if e < 2:

            @pl.when(c == e)
            def _():
                tops_here(e, place).start()

            @pl.when(c != e)
            def _():
                tops_there(e, place, c).start()

        else:
            tops_there(e, place, c).start()
        return result

    def up(place, steps):
        real, imag = uin[place, 0].astype(F32), uin[place, 1].astype(F32)
        for e in reversed(range(steps)):
            real, imag = backward(e, place, real, imag)

    @pl.when(z == last)
    def _():
        uin[...] = jnp.zeros_like(uin)

    @pl.loop(0, chunks)
    def _(place):
        @pl.when(z == 0)
        def _():
            bin_chunk(place)

        @pl.when(z > 0)
        def _():
            for half in range(HALF):
                down_copy(place, half).wait_recv()

        down(place)

        @pl.when(z == last)
        def _():
            up(place, 2)

    @pl.when(z == 2)
    def _():
        lend(0).start()
        lend(1).start()

    def wait_up(place):
        for half in range(HALF):
            up_copy(place, half).wait_recv()

    @pl.when(z == 0)
    def _():
        @pl.loop(0, chunks)
        def _(place):
            wait_up(place)
            up(place, 2)

    @pl.when(host)
    def _():
        for e in range(2, 4):
            par_copy(e, e, 0, partner).wait_recv()
            angles(e)
            oper_copy(opn.at[e], e, partner).wait_recv()

        @pl.loop(0, chunks)
        def _(place):
            again(place)

        @pl.loop(0, chunks)
        def _(place):
            wait_up(place)
            up(place, 4)

    row4 = lax.broadcasted_iota(jnp.int32, (4, 128), 0)

    def rows_tile(summed):
        tile = jnp.zeros((4, 128), F32)
        for q in range(4):
            tile = jnp.where(row4 == q, summed[:, 128 * q : 128 * (q + 1)], tile)
        return tile

    def part_copy(e, sender):
        return pltpu.make_async_remote_copy(
            src_ref=gpart.at[e],
            dst_ref=gin.at[sender],
            send_sem=part_send.at[e],
            recv_sem=part_recv.at[sender],
            device_id=at(base + e),
            device_id_type=MESH,
        )

    def share(steps):
        for e in range(steps):
            gpart[e] = rows_tile(jnp.sum(gacc[e], axis=0, keepdims=True))
            if e < 2:

                @pl.when(c != e)
                def _():
                    part_copy(e, c).start()

            else:
                part_copy(e, c).start()

        part_copy(0, 1 - c).wait_recv()
        gin[c] = gpart[c]

    @pl.when(host)
    def _():
        share(4)

    @pl.when((z == 0) | (z == last))
    def _():
        share(2)

    @pl.when(helper)
    def _():
        part_copy(0, 0).wait_recv()
        part_copy(0, 1).wait_recv()

    total = gin[0] + gin[1]
    gsend[...] = total
    gbox[f] = total

    def g_copy(k):
        return pltpu.make_async_remote_copy(
            src_ref=gsend,
            dst_ref=gbox.at[f],
            send_sem=g_send.at[k],
            recv_sem=g_recv.at[f],
            device_id={"freq": (f + k) % n_freq},
            device_id_type=MESH,
        )

    @pl.loop(1, n_freq)
    def _(k):
        g_copy(k).start()

    @pl.loop(1, n_freq)
    def _(k):
        source = (f + k) % n_freq
        pltpu.make_async_remote_copy(
            src_ref=gsend,
            dst_ref=gbox.at[source],
            send_sem=g_send.at[k],
            recv_sem=g_recv.at[source],
            device_id={"freq": source},
            device_id_type=MESH,
        ).wait_recv()

    total = jnp.sum(gbox[...], axis=0) * (1.0 / (2.0 * n_freq * SHOTS_DEV * n_freq))
    grad_ref[...] = jnp.concatenate([total[q : q + 1] for q in range(4)], axis=1)

    to_partner.wait_send()
    par_copy(c, c, 0, partner).wait_send()

    @pl.when(helper)
    def _():
        par_copy(c, 2 + c, 1, above).wait_send()
        par_copy(c, 2 + c, 2, cross).wait_send()
        lend(0).wait_send()
        lend(1).wait_send()

    @pl.loop(1, n_freq)
    def _(k):
        g_copy(k).wait_send()

    @pl.when(z == 0)
    def _():
        @pl.loop(1, n_freq)
        def _(k):
            box_copy(k).wait_send()

    steps = jnp.where(host, 4, jnp.where(helper, 0, 2))

    @pl.loop(0, steps)
    def _(e):
        @pl.when(c != e)
        def _():
            part_copy(e, c).wait_send()

            @pl.loop(0, chunks)
            def _(place):
                tops_there(e, place, c).wait_send()

    @pl.loop(0, chunks)
    def _(place):
        for half in range(HALF):

            @pl.when(z < last)
            def _():
                down_copy(place, half).wait_send()

            @pl.when((z > 0) & jnp.logical_not(helper))
            def _():
                up_copy(place, half).wait_send()

        tops_there(0, place, 1 - c).wait_recv()

        @pl.when(helper)
        def _():
            tops_there(0, place, c).wait_recv()

        @pl.when(jnp.logical_not(helper))
        def _():
            tops_here(c, place).wait()


def body(traces, shot_of_trace, receiver_cell, slot_freq, operators, slowness, image_model):
    n_freq = lax.axis_size("freq")
    n_depth = lax.axis_size("depth")
    local_freqs = operators.shape[1]
    lateral = operators.shape[-1]
    shot_total = SHOTS_DEV * n_freq
    chunks = shot_total // SH
    block = (2, SH, lateral)
    vmem = pl.BlockSpec(memory_space=pltpu.VMEM)
    dma = pltpu.SemaphoreType.DMA
    gradient, tops = pl.pallas_call(
        functools.partial(kernel, n_depth, n_freq),
        out_shape=(
            jax.ShapeDtypeStruct((1, lateral), F32),
            jax.ShapeDtypeStruct((1, local_freqs, 2, shot_total, lateral), BF16),
        ),
        in_specs=[pl.BlockSpec(memory_space=pltpu.HBM)] * 7,
        out_specs=(vmem, pl.BlockSpec(memory_space=pl.ANY)),
        scratch_shapes=[
            pltpu.SMEM(slot_freq.shape, jnp.int32),
            pltpu.VMEM(traces.shape, BF16),
            pltpu.VMEM(shot_of_trace.shape, jnp.int32),
            pltpu.VMEM(receiver_cell.shape, jnp.int32),
            pltpu.VMEM(slowness.shape, F32),
            pltpu.VMEM(image_model.shape, F32),
            pltpu.VMEM((4, 2, lateral, lateral), BF16),
            pltpu.VMEM((2, 2, lateral, lateral), BF16),
            pltpu.VMEM((4, 8, lateral), F32),
            pltpu.VMEM((4, 1, lateral), F32),
            pltpu.VMEM((4, 1, lateral), F32),
            pltpu.VMEM((n_freq, 16, 128), BF16),
            pltpu.VMEM((n_freq, 16, 128), BF16),
            pltpu.VMEM((8, SH + 32, 128), F32),
            pltpu.VMEM((chunks,) + block, BF16),
            pltpu.VMEM((chunks,) + block, BF16),
            pltpu.VMEM((4, chunks) + block, BF16),
            pltpu.VMEM((chunks,) + block, BF16),
            pltpu.VMEM((4, chunks) + block, BF16),
            pltpu.VMEM((4, 8, lateral), F32),
            pltpu.VMEM((4, 4, 128), F32),
            pltpu.VMEM((2, 4, 128), F32),
            pltpu.VMEM((4, 128), F32),
            pltpu.VMEM((n_freq, 4, 128), F32),
            dma((7,)),
            dma((4,)),
            dma((4,)),
            dma((3,)),
            dma((4,)),
            dma((n_freq,)),
            dma((n_freq,)),
            dma((chunks, HALF)),
            dma((chunks, HALF)),
            dma((chunks, HALF)),
            dma((chunks, HALF)),
            dma((chunks,)),
            dma((4, chunks)),
            dma((2, chunks)),
            dma((4,)),
            dma((2,)),
            dma((n_freq,)),
            dma((n_freq,)),
        ],
        compiler_params=pltpu.CompilerParams(
            collective_id=0, has_side_effects=True, vmem_limit_bytes=60 * 2**20
        ),
        cost_estimate=pl.CostEstimate(flops=2 * 10**9, bytes_accessed=4 * 10**6, transcendentals=4096),
        name="migrate",
    )(slot_freq, traces, shot_of_trace, receiver_cell, slowness, image_model, operators)
    return gradient, tops


def solution(mesh):
    in_specs = (
        P("freq", None),
        P("freq", None),
        P("freq", None),
        P("freq"),
        P("depth", "freq", None, None, None),
        P("depth", None),
        P("depth", None),
    )
    out_specs = (P("depth", None), P("depth", "freq", None, None, None))
    return jax.shard_map(body, mesh=mesh, in_specs=in_specs, out_specs=out_specs, check_vma=False)
```

```python
import functools

import jax
import jax.numpy as jnp
from jax import lax
from jax.experimental import pallas as pl
from jax.experimental.pallas import tpu as pltpu
from jax.sharding import PartitionSpec as P

MESH = pl.DeviceIdType.MESH
SHOTS_DEV = 6
SH = 16
HALF = 1
HOSTS = ()
EARLY = ()
F32 = jnp.float32
BF16 = jnp.bfloat16


def product(rows, matrix):
    return jnp.dot(rows, matrix, preferred_element_type=F32)


def product_rows(rows, matrix):
    return lax.dot_general(rows, matrix, (((1,), (1,)), ((), ())), preferred_element_type=F32)


def lanes(tile, row, width):
    return jnp.concatenate([tile[4 * q + row : 4 * q + row + 1] for q in range(width // 128)], axis=1)


def kernel(
    n_depth,
    n_freq,
    slot_hbm,
    traces_hbm,
    shot_hbm,
    cell_hbm,
    slow_hbm,
    model_hbm,
    oper_ref,
    grad_ref,
    tops_ref,
    slot_ref,
    traces_ref,
    shot_ref,
    cell_ref,
    slow_ref,
    model_ref,
    opn,
    opt,
    par,
    cosines,
    sines,
    outbox,
    inbox,
    bins,
    din,
    dout,
    vbuf,
    uin,
    abuf,
    gacc,
    gpart,
    gin,
    gsend,
    gbox,
    load_sem,
    oper_send,
    oper_recv,
    par_send,
    par_recv,
    box_send,
    box_recv,
    down_send,
    down_recv,
    up_send,
    up_recv,
    tops_local,
    tops_send,
    tops_recv,
    part_send,
    part_recv,
    g_send,
    g_recv,
):
    d = lax.axis_index("depth")
    f = lax.axis_index("freq")
    z = d // 2
    c = d % 2
    chunks = din.shape[0]
    lateral = din.shape[-1]
    last = n_depth // 2 - 1

    def among(chips, shift=0):
        found = z < 0
        for chip in chips:
            found = found | (z == chip + shift)
        return found

    host = among(HOSTS)
    helper = among(HOSTS, 1)
    early = among(EARLY, 1)
    skips = among(HOSTS, 2)
    base = 2 * z
    partner = base + 1 - c
    cross = jnp.where(host, d + 2, d - 2) + 1 - 2 * c

    def at(depth):
        return {"depth": depth}

    first_chunk = (f * SHOTS_DEV) // SH

    def chunk_of(place):
        return (first_chunk + place) % chunks

    below = (d + 2) % n_depth
    above = (d + n_depth - 2) % n_depth
    up_target = jnp.where(skips, (d + n_depth - 4) % n_depth, above)

    barrier = pltpu.get_barrier_semaphore()

    def greet(depth):
        pl.semaphore_signal(barrier, inc=1, device_id=at(depth), device_id_type=MESH)

    @pl.loop(1, n_freq)
    def _(k):
        pl.semaphore_signal(barrier, inc=1, device_id={"freq": (f + k) % n_freq}, device_id_type=MESH)

    greet(partner)

    @pl.when(z > 0)
    def _():
        greet(above)

    @pl.when(z < last)
    def _():
        greet(below)

    @pl.when(host)
    def _():
        greet((d + 4) % n_depth)

    @pl.when(skips)
    def _():
        greet(up_target)

    @pl.when(host | helper)
    def _():
        greet(cross)

    greeted = (
        n_freq
        + jnp.where(z > 0, 1, 0)
        + jnp.where(z < last, 1, 0)
        + jnp.where(host, 1, 0)
        + jnp.where(skips, 1, 0)
        + jnp.where(host | helper, 1, 0)
    )

    loads = [
        pltpu.make_async_copy(source, target, load_sem.at[i])
        for i, (source, target) in enumerate(
            [
                (slow_hbm, slow_ref),
                (model_hbm, model_ref),
                (slot_hbm, slot_ref),
                (traces_hbm, traces_ref),
                (shot_hbm, shot_ref),
                (cell_hbm, cell_ref),
                (oper_ref.at[0, c], opn.at[c]),
            ]
        )
    ]

    @pl.when(z == 0)
    def _():
        for load in loads[3:6]:
            load.start()

    for load in loads[:3] + loads[6:]:
        load.start()
    for load in loads[:2]:
        load.wait()

    row8 = lax.broadcasted_iota(jnp.int32, (8, lateral), 0)
    par[c] = jnp.where(row8 == 0, slow_ref[...], model_ref[...])

    @pl.when(z == 0)
    def _():
        for load in loads[3:6]:
            load.wait()
        rows = n_freq * 16
        row = lax.broadcasted_iota(jnp.int32, (rows, 128), 0)
        column = lax.broadcasted_iota(jnp.int32, (rows, 128), 1)
        group, within = row // 16, row % 16
        kind, piece = within % 4, within // 4
        wanted = jnp.where(kind < 2, group * 4 + 2 * c + kind, -1)
        total = jnp.zeros((rows, 128), F32)
        for q in range(4):
            select = jnp.where((column == wanted) & (piece == q), 1.0, 0.0).astype(BF16)
            total += lax.dot_general(
                select,
                traces_ref[128 * q : 128 * (q + 1), :],
                (((1,), (1,)), ((), ())),
                preferred_element_type=F32,
            )
        cell = cell_ref[...]
        first = (cell // 128 * 8 + shot_ref[...]).astype(F32)
        second = (cell % 128).astype(F32)
        row16 = lax.broadcasted_iota(jnp.int32, (16, 128), 0)
        label = jnp.zeros((16, 128), F32)
        for q in range(4):
            label = jnp.where(row16 == 4 * q + 2, first[:, 128 * q : 128 * (q + 1)], label)
            label = jnp.where(row16 == 4 * q + 3, second[:, 128 * q : 128 * (q + 1)], label)
        filled = total.reshape(n_freq, 16, 128) + label[None]
        outbox[...] = filled.astype(BF16)
        inbox[f] = outbox[f]

    pl.semaphore_wait(barrier, greeted)

    def box_copy(k):
        return pltpu.make_async_remote_copy(
            src_ref=outbox.at[(f + k) % n_freq],
            dst_ref=inbox.at[f],
            send_sem=box_send.at[k],
            recv_sem=box_recv.at[f],
            device_id={"freq": (f + k) % n_freq},
            device_id_type=MESH,
        )

    @pl.when(z == 0)
    def _():
        @pl.loop(1, n_freq // 2)
        def _(k):
            box_copy(k).start()
            box_copy(n_freq - k).start()

        box_copy(n_freq // 2).start()

    def par_copy(index, place, send, target):
        return pltpu.make_async_remote_copy(
            src_ref=par.at[index],
            dst_ref=par.at[place],
            send_sem=par_send.at[send],
            recv_sem=par_recv.at[place],
            device_id=at(target),
            device_id_type=MESH,
        )

    def oper_copy(source, place, target):
        return pltpu.make_async_remote_copy(
            src_ref=source,
            dst_ref=opn.at[place],
            send_sem=oper_send.at[place],
            recv_sem=oper_recv.at[place],
            device_id=at(target),
            device_id_type=MESH,
        )

    to_partner = oper_copy(oper_ref.at[0, 1 - c], c, partner)
    to_partner.start()
    par_copy(c, c, 0, partner).start()

    @pl.when(helper)
    def _():
        par_copy(c, 2 + c, 1, above).start()
        par_copy(c, 2 + c, 2, cross).start()

    def lend(e):
        return oper_copy(opn.at[e], 2 + e, above)

    loads[2].wait()
    loads[6].wait()
    scale = 0.1 * (slot_ref[c].astype(F32) + 1.0)

    def angles(e):
        theta = scale * par[e, 0:1, :]
        cosines[e] = jnp.cos(theta)
        sines[e] = jnp.sin(theta)

    @pl.when(early)
    def _():
        lend(c).start()

    gacc[...] = jnp.zeros_like(gacc)
    for p in range(2):
        opt[c, p] = opn[c, p].T
    par_copy(1 - c, 1 - c, 0, partner).wait_recv()
    angles(0)
    angles(1)
    oper_copy(oper_ref.at[0, c], 1 - c, partner).wait_recv()

    @pl.when(early)
    def _():
        lend(1 - c).start()

    for p in range(2):
        opt[1 - c, p] = opn[1 - c, p].T

    def wait_box(source):
        @pl.when(source != f)
        def _():
            pltpu.make_async_remote_copy(
                src_ref=outbox.at[source],
                dst_ref=inbox.at[source],
                send_sem=box_send.at[source],
                recv_sem=box_recv.at[source],
                device_id={"freq": source},
                device_id_type=MESH,
            ).wait_recv()

    counts = [(SH * j + SH - 1) // SHOTS_DEV - SH * j // SHOTS_DEV + 1 for j in range(chunks)]
    fewest, most = min(counts), max(counts)

    def bin_chunk(place):
        j = chunk_of(place)
        start = SH * j
        first_source = start // SHOTS_DEV
        fresh = jnp.where(place == 0, first_source, (start + SHOTS_DEV - 1) // SHOTS_DEV)
        after = jnp.where(
            (place == chunks - 1) & (first_chunk > 0),
            (SH * first_chunk) // SHOTS_DEV,
            (start + SH - 1) // SHOTS_DEV + 1,
        )

        @pl.loop(fresh, after)
        def _(source):
            wait_box(source)

        top = 8 + SHOTS_DEV * first_source - start
        row = lax.broadcasted_iota(jnp.int32, (32, 4 * 128), 0).astype(F32)
        lane_row = lax.broadcasted_iota(jnp.int32, (128, 4 * 128), 0).astype(F32)

        def add_source(i):
            tile = inbox[first_source + i].astype(F32)
            real, imag = lanes(tile, 0, 512), lanes(tile, 1, 512)
            first, low = lanes(tile, 2, 512), lanes(tile, 3, 512)
            hit = row == first
            left = jnp.concatenate(
                [jnp.where(hit, real, 0.0).astype(BF16), jnp.where(hit, imag, 0.0).astype(BF16)], axis=0
            )
            right = jnp.where(lane_row == low, 1.0, 0.0).astype(BF16)
            part = lax.dot_general(left, right, (((1,), (1,)), ((), ())), preferred_element_type=F32)
            for g in range(8):
                bins[g, pl.ds(top + SHOTS_DEV * i, 8), :] = part[8 * g : 8 * (g + 1)]

        for i in range(fewest):
            add_source(i)

        for i in range(fewest, most):

            @pl.when(first_source + i <= (start + SH - 1) // SHOTS_DEV)
            def _():
                add_source(i)

        for p in range(2):
            for high in range(4):
                din[place, p, :, 128 * high : 128 * (high + 1)] = bins[4 * p + high, 8 : 8 + SH, :].astype(BF16)

    def columns(half):
        width = lateral // HALF
        return pl.ds(half * width, width)

    def down_copy(place, half):
        return pltpu.make_async_remote_copy(
            src_ref=dout.at[place, :, :, columns(half)],
            dst_ref=din.at[place, :, :, columns(half)],
            send_sem=down_send.at[place, half],
            recv_sem=down_recv.at[place, half],
            device_id=at(below),
            device_id_type=MESH,
        )

    def up_copy(place, half):
        return pltpu.make_async_remote_copy(
            src_ref=abuf.at[0, place, :, :, columns(half)],
            dst_ref=uin.at[place, :, :, columns(half)],
            send_sem=up_send.at[place, half],
            recv_sem=up_recv.at[place, half],
            device_id=at(up_target),
            device_id_type=MESH,
        )

    def shift(e, place, real, imag):
        cos_row, sin_row = cosines[e], sines[e]
        shifted_real = (cos_row * real - sin_row * imag).astype(BF16)
        shifted_imag = (cos_row * imag + sin_row * real).astype(BF16)
        vbuf[e, place, 0] = shifted_real
        vbuf[e, place, 1] = shifted_imag
        return jnp.concatenate([shifted_real, shifted_imag], axis=0)

    def forward(stacked, by_real, by_imag):
        return (by_real[:SH] - by_imag[SH:]).astype(BF16), (by_imag[:SH] + by_real[SH:]).astype(BF16)

    def down(place):
        stacked = shift(0, place, din[place, 0].astype(F32), din[place, 1].astype(F32))
        real, imag = forward(stacked, product(stacked, opt[0, 0]), product(stacked, opt[0, 1]))
        stacked = shift(1, place, real.astype(F32), imag.astype(F32))

        @pl.when(z < last)
        def _():
            for half in range(HALF):
                cols = columns(half)
                real, imag = forward(
                    stacked, product(stacked, opt[1, 0, :, cols]), product(stacked, opt[1, 1, :, cols])
                )
                dout[place, 0, :, cols] = real
                dout[place, 1, :, cols] = imag
                down_copy(place, half).start()

    def again(place):
        stacked = shift(2, place, dout[place, 0].astype(F32), dout[place, 1].astype(F32))
        real, imag = forward(stacked, product_rows(stacked, opn[2, 0]), product_rows(stacked, opn[2, 1]))
        shift(3, place, real.astype(F32), imag.astype(F32))

    def rows_of(place):
        return pl.ds(pl.multiple_of(chunk_of(place) * SH, SH), SH)

    def tops_here(e, place):
        return pltpu.make_async_copy(abuf.at[e, place], tops_ref.at[0, c, :, rows_of(place), :], tops_local.at[place])

    def tops_there(e, place, its_slot):
        return pltpu.make_async_remote_copy(
            src_ref=abuf.at[e, place],
            dst_ref=tops_ref.at[0, its_slot, :, rows_of(place), :],
            send_sem=tops_send.at[e, place],
            recv_sem=tops_recv.at[its_slot, place],
            device_id=at(base + e),
            device_id_type=MESH,
        )

    def backward(e, place, real, imag):
        old_real, old_imag = vbuf[e, place, 0].astype(F32), vbuf[e, place, 1].astype(F32)
        model = par[e, 1:2, :]
        source_real = real + model * old_real
        source_imag = imag + model * old_imag
        term = old_real * source_real + old_imag * source_imag
        gacc[e] += jnp.sum(term.reshape(SH // 8, 8, lateral), axis=0)
        stacked = jnp.concatenate([source_real.astype(BF16), source_imag.astype(BF16)], axis=0)
        pieces = HALF if e == 0 else 1
        width = lateral // pieces
        result = []
        for piece in range(pieces):
            cols = pl.ds(piece * width, width)
            by_real = product(stacked, opn[e, 0, :, cols])
            by_imag = product(stacked, opn[e, 1, :, cols])
            back_real = by_real[:SH] + by_imag[SH:]
            back_imag = by_real[SH:] - by_imag[:SH]
            cos_row, sin_row = cosines[e, :, cols], sines[e, :, cols]
            out_real = (cos_row * back_real + sin_row * back_imag).astype(BF16)
            out_imag = (cos_row * back_imag - sin_row * back_real).astype(BF16)
            abuf[e, place, 0, :, cols] = out_real
            abuf[e, place, 1, :, cols] = out_imag
            result = out_real.astype(F32), out_imag.astype(F32)
            if e == 0:

                @pl.when(z > 0)
                def _():
                    up_copy(place, piece).start()

        if e < 2:

            @pl.when(c == e)
            def _():
                tops_here(e, place).start()

            @pl.when(c != e)
            def _():
                tops_there(e, place, c).start()

        else:
            tops_there(e, place, c).start()
        return result

    def up(place, steps):
        real, imag = uin[place, 0].astype(F32), uin[place, 1].astype(F32)
        for e in reversed(range(steps)):
            real, imag = backward(e, place, real, imag)

    @pl.when(z == last)
    def _():
        uin[...] = jnp.zeros_like(uin)

    @pl.loop(0, chunks)
    def _(place):
        @pl.when(z == 0)
        def _():
            bin_chunk(place)

        @pl.when(z > 0)
        def _():
            for half in range(HALF):
                down_copy(place, half).wait_recv()

        down(place)

        @pl.when(z == last)
        def _():
            up(place, 2)

    @pl.when(helper & jnp.logical_not(early))
    def _():
        lend(0).start()
        lend(1).start()

    def wait_up(place):
        for half in range(HALF):
            up_copy(place, half).wait_recv()

    plain = jnp.logical_not(host | helper)

    @pl.when(plain & (z < last))
    def _():
        @pl.loop(0, chunks)
        def _(place):
            wait_up(place)
            up(place, 2)

    @pl.when(host)
    def _():
        for e in range(2, 4):
            par_copy(e, e, 0, partner).wait_recv()
            angles(e)
            oper_copy(opn.at[e], e, partner).wait_recv()

        @pl.loop(0, chunks)
        def _(place):
            again(place)

        @pl.loop(0, chunks)
        def _(place):
            wait_up(place)
            up(place, 4)

    row4 = lax.broadcasted_iota(jnp.int32, (4, 128), 0)

    def rows_tile(summed):
        tile = jnp.zeros((4, 128), F32)
        for q in range(4):
            tile = jnp.where(row4 == q, summed[:, 128 * q : 128 * (q + 1)], tile)
        return tile

    def part_copy(e, sender):
        return pltpu.make_async_remote_copy(
            src_ref=gpart.at[e],
            dst_ref=gin.at[sender],
            send_sem=part_send.at[e],
            recv_sem=part_recv.at[sender],
            device_id=at(base + e),
            device_id_type=MESH,
        )

    def share(steps):
        for e in range(steps):
            gpart[e] = rows_tile(jnp.sum(gacc[e], axis=0, keepdims=True))
            if e < 2:

                @pl.when(c != e)
                def _():
                    part_copy(e, c).start()

            else:
                part_copy(e, c).start()

        part_copy(0, 1 - c).wait_recv()
        gin[c] = gpart[c]

    @pl.when(host)
    def _():
        share(4)

    @pl.when(plain)
    def _():
        share(2)

    @pl.when(helper)
    def _():
        part_copy(0, 0).wait_recv()
        part_copy(0, 1).wait_recv()

    total = gin[0] + gin[1]
    gsend[...] = total
    gbox[f] = total

    def g_copy(k):
        return pltpu.make_async_remote_copy(
            src_ref=gsend,
            dst_ref=gbox.at[f],
            send_sem=g_send.at[k],
            recv_sem=g_recv.at[f],
            device_id={"freq": (f + k) % n_freq},
            device_id_type=MESH,
        )

    @pl.loop(1, n_freq)
    def _(k):
        g_copy(k).start()

    @pl.loop(1, n_freq)
    def _(k):
        source = (f + k) % n_freq
        pltpu.make_async_remote_copy(
            src_ref=gsend,
            dst_ref=gbox.at[source],
            send_sem=g_send.at[k],
            recv_sem=g_recv.at[source],
            device_id={"freq": source},
            device_id_type=MESH,
        ).wait_recv()

    total = jnp.sum(gbox[...], axis=0) * (1.0 / (2.0 * n_freq * SHOTS_DEV * n_freq))
    grad_ref[...] = jnp.concatenate([total[q : q + 1] for q in range(4)], axis=1)

    to_partner.wait_send()
    par_copy(c, c, 0, partner).wait_send()

    @pl.when(helper)
    def _():
        par_copy(c, 2 + c, 1, above).wait_send()
        par_copy(c, 2 + c, 2, cross).wait_send()
        lend(0).wait_send()
        lend(1).wait_send()

    @pl.loop(1, n_freq)
    def _(k):
        g_copy(k).wait_send()

    @pl.when(z == 0)
    def _():
        @pl.loop(1, n_freq)
        def _(k):
            box_copy(k).wait_send()

    steps = jnp.where(host, 4, jnp.where(helper, 0, 2))

    @pl.loop(0, steps)
    def _(e):
        @pl.when(c != e)
        def _():
            part_copy(e, c).wait_send()

            @pl.loop(0, chunks)
            def _(place):
                tops_there(e, place, c).wait_send()

    @pl.loop(0, chunks)
    def _(place):
        for half in range(HALF):

            @pl.when(z < last)
            def _():
                down_copy(place, half).wait_send()

            @pl.when((z > 0) & jnp.logical_not(helper))
            def _():
                up_copy(place, half).wait_send()

        tops_there(0, place, 1 - c).wait_recv()

        @pl.when(helper)
        def _():
            tops_there(0, place, c).wait_recv()

        @pl.when(jnp.logical_not(helper))
        def _():
            tops_here(c, place).wait()


def body(traces, shot_of_trace, receiver_cell, slot_freq, operators, slowness, image_model):
    n_freq = lax.axis_size("freq")
    n_depth = lax.axis_size("depth")
    local_freqs = operators.shape[1]
    lateral = operators.shape[-1]
    shot_total = SHOTS_DEV * n_freq
    chunks = shot_total // SH
    block = (2, SH, lateral)
    vmem = pl.BlockSpec(memory_space=pltpu.VMEM)
    dma = pltpu.SemaphoreType.DMA
    gradient, tops = pl.pallas_call(
        functools.partial(kernel, n_depth, n_freq),
        out_shape=(
            jax.ShapeDtypeStruct((1, lateral), F32),
            jax.ShapeDtypeStruct((1, local_freqs, 2, shot_total, lateral), BF16),
        ),
        in_specs=[pl.BlockSpec(memory_space=pltpu.HBM)] * 7,
        out_specs=(vmem, pl.BlockSpec(memory_space=pl.ANY)),
        scratch_shapes=[
            pltpu.SMEM(slot_freq.shape, jnp.int32),
            pltpu.VMEM(traces.shape, BF16),
            pltpu.VMEM(shot_of_trace.shape, jnp.int32),
            pltpu.VMEM(receiver_cell.shape, jnp.int32),
            pltpu.VMEM(slowness.shape, F32),
            pltpu.VMEM(image_model.shape, F32),
            pltpu.VMEM((4, 2, lateral, lateral), BF16),
            pltpu.VMEM((2, 2, lateral, lateral), BF16),
            pltpu.VMEM((4, 8, lateral), F32),
            pltpu.VMEM((4, 1, lateral), F32),
            pltpu.VMEM((4, 1, lateral), F32),
            pltpu.VMEM((n_freq, 16, 128), BF16),
            pltpu.VMEM((n_freq, 16, 128), BF16),
            pltpu.VMEM((8, SH + 32, 128), F32),
            pltpu.VMEM((chunks,) + block, BF16),
            pltpu.VMEM((chunks,) + block, BF16),
            pltpu.VMEM((4, chunks) + block, BF16),
            pltpu.VMEM((chunks,) + block, BF16),
            pltpu.VMEM((4, chunks) + block, BF16),
            pltpu.VMEM((4, 8, lateral), F32),
            pltpu.VMEM((4, 4, 128), F32),
            pltpu.VMEM((2, 4, 128), F32),
            pltpu.VMEM((4, 128), F32),
            pltpu.VMEM((n_freq, 4, 128), F32),
            dma((7,)),
            dma((4,)),
            dma((4,)),
            dma((3,)),
            dma((4,)),
            dma((n_freq,)),
            dma((n_freq,)),
            dma((chunks, HALF)),
            dma((chunks, HALF)),
            dma((chunks, HALF)),
            dma((chunks, HALF)),
            dma((chunks,)),
            dma((4, chunks)),
            dma((2, chunks)),
            dma((4,)),
            dma((2,)),
            dma((n_freq,)),
            dma((n_freq,)),
        ],
        compiler_params=pltpu.CompilerParams(
            collective_id=0, has_side_effects=True, vmem_limit_bytes=60 * 2**20
        ),
        cost_estimate=pl.CostEstimate(flops=2 * 10**9, bytes_accessed=4 * 10**6, transcendentals=4096),
        name="migrate",
    )(slot_freq, traces, shot_of_trace, receiver_cell, slowness, image_model, operators)
    return gradient, tops


def solution(mesh):
    in_specs = (
        P("freq", None),
        P("freq", None),
        P("freq", None),
        P("freq"),
        P("depth", "freq", None, None, None),
        P("depth", None),
        P("depth", None),
    )
    out_specs = (P("depth", None), P("depth", "freq", None, None, None))
    return jax.shard_map(body, mesh=mesh, in_specs=in_specs, out_specs=out_specs, check_vma=False)
```

```python
import functools

import jax
import jax.numpy as jnp
from jax import lax
from jax.experimental import pallas as pl
from jax.experimental.pallas import tpu as pltpu
from jax.sharding import PartitionSpec as P

MESH = pl.DeviceIdType.MESH
SHOTS_DEV = 6
SH = 16
F32 = jnp.float32
BF16 = jnp.bfloat16


def product(rows, matrix):
    return jnp.dot(rows, matrix, preferred_element_type=F32)


def lanes(tile, row, width):
    return jnp.concatenate([tile[4 * q + row : 4 * q + row + 1] for q in range(width // 128)], axis=1)


def kernel(
    n_depth,
    n_freq,
    slot_hbm,
    traces_hbm,
    shot_hbm,
    cell_hbm,
    slow_hbm,
    model_hbm,
    oper_ref,
    grad_ref,
    tops_ref,
    slot_ref,
    traces_ref,
    shot_ref,
    cell_ref,
    slow_ref,
    model_ref,
    opn,
    opt,
    par,
    cosines,
    sines,
    outbox,
    inbox,
    bins,
    din,
    dout,
    vbuf,
    uin,
    abuf,
    gacc,
    gpart,
    gin,
    gsend,
    gbox,
    load_sem,
    oper_send,
    oper_recv,
    par_send,
    par_recv,
    box_send,
    box_recv,
    down_send,
    down_recv,
    up_send,
    up_recv,
    tops_local,
    tops_send,
    tops_recv,
    part_send,
    part_recv,
    g_send,
    g_recv,
):
    d = lax.axis_index("depth")
    f = lax.axis_index("freq")
    z = d // 2
    c = d % 2
    chunks = din.shape[0]
    lateral = din.shape[-1]
    last = n_depth // 2 - 1
    base = 2 * z
    partner = base + 1 - c

    def at(depth):
        return {"depth": depth}

    first_chunk = (f * SHOTS_DEV) // SH

    def chunk_of(place):
        return (first_chunk + place) % chunks

    below = (d + 2) % n_depth
    above = (d + n_depth - 2) % n_depth

    barrier = pltpu.get_barrier_semaphore()

    def greet(depth):
        pl.semaphore_signal(barrier, inc=1, device_id=at(depth), device_id_type=MESH)

    def greet_group(k):
        pl.semaphore_signal(barrier, inc=1, device_id={"freq": (f + k) % n_freq}, device_id_type=MESH)

    greet_group(n_freq // 2)

    @pl.loop(1, n_freq // 2)
    def _(k):
        greet_group(n_freq // 2 + k)
        greet_group(n_freq // 2 - k)

    greet(partner)

    @pl.when(z > 0)
    def _():
        greet(above)

    @pl.when(z < last)
    def _():
        greet(below)

    greeted = n_freq + jnp.where(z > 0, 1, 0) + jnp.where(z < last, 1, 0)

    loads = [
        pltpu.make_async_copy(source, target, load_sem.at[i])
        for i, (source, target) in enumerate(
            [
                (slow_hbm, slow_ref),
                (model_hbm, model_ref),
                (slot_hbm, slot_ref),
                (traces_hbm, traces_ref),
                (shot_hbm, shot_ref),
                (cell_hbm, cell_ref),
                (oper_ref.at[0, c], opn.at[c]),
            ]
        )
    ]

    @pl.when(z == 0)
    def _():
        for load in loads[3:6]:
            load.start()

    for load in loads[:3] + loads[6:]:
        load.start()
    for load in loads[:2]:
        load.wait()

    row8 = lax.broadcasted_iota(jnp.int32, (8, lateral), 0)
    par[c] = jnp.where(row8 == 0, slow_ref[...], model_ref[...])

    @pl.when(z == 0)
    def _():
        for load in loads[3:6]:
            load.wait()
        rows = n_freq * 16
        row = lax.broadcasted_iota(jnp.int32, (rows, 128), 0)
        column = lax.broadcasted_iota(jnp.int32, (rows, 128), 1)
        group, within = row // 16, row % 16
        kind, piece = within % 4, within // 4
        wanted = jnp.where(kind < 2, group * 4 + 2 * c + kind, -1)
        total = jnp.zeros((rows, 128), F32)
        for q in range(4):
            select = jnp.where((column == wanted) & (piece == q), 1.0, 0.0).astype(BF16)
            total += lax.dot_general(
                select,
                traces_ref[128 * q : 128 * (q + 1), :],
                (((1,), (1,)), ((), ())),
                preferred_element_type=F32,
            )
        cell = cell_ref[...]
        first = (cell // 128 * 8 + shot_ref[...]).astype(F32)
        second = (cell % 128).astype(F32)
        row16 = lax.broadcasted_iota(jnp.int32, (16, 128), 0)
        label = jnp.zeros((16, 128), F32)
        for q in range(4):
            label = jnp.where(row16 == 4 * q + 2, first[:, 128 * q : 128 * (q + 1)], label)
            label = jnp.where(row16 == 4 * q + 3, second[:, 128 * q : 128 * (q + 1)], label)
        filled = total.reshape(n_freq, 16, 128) + label[None]
        outbox[...] = filled.astype(BF16)
        inbox[f] = outbox[f]

    pl.semaphore_wait(barrier, greeted)

    def box_copy(k):
        return pltpu.make_async_remote_copy(
            src_ref=outbox.at[(f + k) % n_freq],
            dst_ref=inbox.at[f],
            send_sem=box_send.at[k],
            recv_sem=box_recv.at[f],
            device_id={"freq": (f + k) % n_freq},
            device_id_type=MESH,
        )

    @pl.when(z == 0)
    def _():
        @pl.loop(1, n_freq // 2)
        def _(k):
            box_copy(k).start()
            box_copy(n_freq - k).start()

        box_copy(n_freq // 2).start()

    def par_copy(index):
        return pltpu.make_async_remote_copy(
            src_ref=par.at[index],
            dst_ref=par.at[index],
            send_sem=par_send,
            recv_sem=par_recv,
            device_id=at(partner),
            device_id_type=MESH,
        )

    def oper_copy(slot, index):
        return pltpu.make_async_remote_copy(
            src_ref=oper_ref.at[0, slot],
            dst_ref=opn.at[index],
            send_sem=oper_send,
            recv_sem=oper_recv,
            device_id=at(partner),
            device_id_type=MESH,
        )

    oper_copy(1 - c, c).start()
    par_copy(c).start()

    loads[2].wait()
    loads[6].wait()
    scale = 0.1 * (slot_ref[c].astype(F32) + 1.0)

    def angles(e):
        theta = scale * par[e, 0:1, :]
        cosines[e] = jnp.cos(theta)
        sines[e] = jnp.sin(theta)

    gacc[...] = jnp.zeros_like(gacc)
    for p in range(2):
        opt[c, p] = opn[c, p].T
    par_copy(1 - c).wait_recv()
    angles(0)
    angles(1)
    oper_copy(c, 1 - c).wait_recv()

    for p in range(2):
        opt[1 - c, p] = opn[1 - c, p].T

    def wait_box(source):
        @pl.when(source != f)
        def _():
            pltpu.make_async_remote_copy(
                src_ref=outbox.at[source],
                dst_ref=inbox.at[source],
                send_sem=box_send.at[source],
                recv_sem=box_recv.at[source],
                device_id={"freq": source},
                device_id_type=MESH,
            ).wait_recv()

    counts = [(SH * j + SH - 1) // SHOTS_DEV - SH * j // SHOTS_DEV + 1 for j in range(chunks)]
    fewest, most = min(counts), max(counts)

    def bin_chunk(place):
        j = chunk_of(place)
        start = SH * j
        first_source = start // SHOTS_DEV
        fresh = jnp.where(place == 0, first_source, (start + SHOTS_DEV - 1) // SHOTS_DEV)
        after = jnp.where(
            (place == chunks - 1) & (first_chunk > 0),
            (SH * first_chunk) // SHOTS_DEV,
            (start + SH - 1) // SHOTS_DEV + 1,
        )

        @pl.loop(fresh, after)
        def _(source):
            wait_box(source)

        top = 8 + SHOTS_DEV * first_source - start
        row = lax.broadcasted_iota(jnp.int32, (32, 4 * 128), 0).astype(F32)
        lane_row = lax.broadcasted_iota(jnp.int32, (128, 4 * 128), 0).astype(F32)

        def add_source(i):
            tile = inbox[first_source + i].astype(F32)
            real, imag = lanes(tile, 0, 512), lanes(tile, 1, 512)
            first, low = lanes(tile, 2, 512), lanes(tile, 3, 512)
            hit = row == first
            left = jnp.concatenate(
                [jnp.where(hit, real, 0.0).astype(BF16), jnp.where(hit, imag, 0.0).astype(BF16)], axis=0
            )
            right = jnp.where(lane_row == low, 1.0, 0.0).astype(BF16)
            part = lax.dot_general(left, right, (((1,), (1,)), ((), ())), preferred_element_type=F32)
            for g in range(8):
                bins[g, pl.ds(top + SHOTS_DEV * i, 8), :] = part[8 * g : 8 * (g + 1)]

        for i in range(fewest):
            add_source(i)

        for i in range(fewest, most):

            @pl.when(first_source + i <= (start + SH - 1) // SHOTS_DEV)
            def _():
                add_source(i)

        for p in range(2):
            for high in range(4):
                din[place, p, :, 128 * high : 128 * (high + 1)] = bins[4 * p + high, 8 : 8 + SH, :].astype(BF16)

    def down_copy(place):
        return pltpu.make_async_remote_copy(
            src_ref=dout.at[place],
            dst_ref=din.at[place],
            send_sem=down_send.at[place],
            recv_sem=down_recv.at[place],
            device_id=at(below),
            device_id_type=MESH,
        )

    def up_copy(place):
        return pltpu.make_async_remote_copy(
            src_ref=abuf.at[0, place],
            dst_ref=uin.at[place],
            send_sem=up_send.at[place],
            recv_sem=up_recv.at[place],
            device_id=at(above),
            device_id_type=MESH,
        )

    def load(ref, place, n):
        return [ref[pl.ds(place, n), p].reshape(n * SH, lateral).astype(F32) for p in range(2)]

    def store(ref, place, n, real, imag):
        ref[pl.ds(place, n), 0] = real.reshape(n, SH, lateral)
        ref[pl.ds(place, n), 1] = imag.reshape(n, SH, lateral)

    def shift(e, place, n, real, imag):
        cos_row, sin_row = cosines[e], sines[e]
        shifted_real = (cos_row * real - sin_row * imag).astype(BF16)
        shifted_imag = (cos_row * imag + sin_row * real).astype(BF16)
        store(vbuf.at[e], place, n, shifted_real, shifted_imag)
        return jnp.concatenate([shifted_real, shifted_imag], axis=0)

    def forward(e, stacked):
        rows = stacked.shape[0] // 2
        by_real, by_imag = product(stacked, opt[e, 0]), product(stacked, opt[e, 1])
        return (by_real[:rows] - by_imag[rows:]).astype(BF16), (by_imag[:rows] + by_real[rows:]).astype(BF16)

    def down(place, n, send):
        stacked = shift(0, place, n, *load(din, place, n))
        real, imag = forward(0, stacked)
        stacked = shift(1, place, n, real.astype(F32), imag.astype(F32))
        if send:
            real, imag = forward(1, stacked)
            store(dout, place, n, real, imag)
            for i in range(n):
                down_copy(place + i).start()

    def rows_of(place):
        return pl.ds(pl.multiple_of(chunk_of(place) * SH, SH), SH)

    def tops_here(e, place):
        return pltpu.make_async_copy(abuf.at[e, place], tops_ref.at[0, c, :, rows_of(place), :], tops_local.at[place])

    def tops_there(e, place, its_slot):
        return pltpu.make_async_remote_copy(
            src_ref=abuf.at[e, place],
            dst_ref=tops_ref.at[0, its_slot, :, rows_of(place), :],
            send_sem=tops_send.at[place],
            recv_sem=tops_recv.at[place],
            device_id=at(partner),
            device_id_type=MESH,
        )

    def backward(e, place, n, real, imag):
        rows = n * SH
        old_real, old_imag = load(vbuf.at[e], place, n)
        model = par[e, 1:2, :]
        source_real = real + model * old_real
        source_imag = imag + model * old_imag
        term = old_real * source_real + old_imag * source_imag
        gacc[e] += jnp.sum(term.reshape(rows // 8, 8, lateral), axis=0)
        stacked = jnp.concatenate([source_real.astype(BF16), source_imag.astype(BF16)], axis=0)
        by_real = product(stacked, opn[e, 0])
        by_imag = product(stacked, opn[e, 1])
        back_real = by_real[:rows] + by_imag[rows:]
        back_imag = by_real[rows:] - by_imag[:rows]
        cos_row, sin_row = cosines[e], sines[e]
        out_real = (cos_row * back_real + sin_row * back_imag).astype(BF16)
        out_imag = (cos_row * back_imag - sin_row * back_real).astype(BF16)
        store(abuf.at[e], place, n, out_real, out_imag)
        for i in range(n):
            if e == 0:

                @pl.when(z > 0)
                def _():
                    up_copy(place + i).start()

            @pl.when(c == e)
            def _():
                tops_here(e, place + i).start()

            @pl.when(c != e)
            def _():
                tops_there(e, place + i, c).start()

        return out_real.astype(F32), out_imag.astype(F32)

    def up(place, n, real, imag):
        real, imag = backward(1, place, n, real, imag)
        backward(0, place, n, real, imag)

    @pl.when(z == 0)
    def _():
        bin_chunk(0)
        down(0, 1, True)

        @pl.loop(0, (chunks - 2) // 2)
        def _(turn):
            place = 1 + 2 * turn
            bin_chunk(place)
            bin_chunk(place + 1)
            down(place, 2, True)

        bin_chunk(chunks - 1)
        down(chunks - 1, 1, True)

    @pl.when((z > 0) & (z < last))
    def _():
        @pl.loop(0, chunks)
        def _(place):
            down_copy(place).wait_recv()
            down(place, 1, True)

    @pl.when(z == last)
    def _():
        def turn_round(place, n):
            for i in range(n):
                down_copy(place + i).wait_recv()
            down(place, n, False)
            nothing = jnp.zeros((n * SH, lateral), F32)
            up(place, n, nothing, nothing)

        @pl.loop(0, (chunks - 2) // 2)
        def _(turn):
            turn_round(2 * turn, 2)

        @pl.loop(chunks - 2, chunks)
        def _(place):
            turn_round(place, 1)

    @pl.when(z < last)
    def _():
        @pl.loop(0, chunks)
        def _(place):
            up_copy(place).wait_recv()
            up(place, 1, *load(uin, place, 1))

    row4 = lax.broadcasted_iota(jnp.int32, (4, 128), 0)

    def rows_tile(summed):
        tile = jnp.zeros((4, 128), F32)
        for q in range(4):
            tile = jnp.where(row4 == q, summed[:, 128 * q : 128 * (q + 1)], tile)
        return tile

    def part_copy(e, sender):
        return pltpu.make_async_remote_copy(
            src_ref=gpart.at[e],
            dst_ref=gin.at[sender],
            send_sem=part_send,
            recv_sem=part_recv,
            device_id=at(partner),
            device_id_type=MESH,
        )

    for e in range(2):
        gpart[e] = rows_tile(jnp.sum(gacc[e], axis=0, keepdims=True))

        @pl.when(c != e)
        def _():
            part_copy(e, c).start()

    part_copy(0, 1 - c).wait_recv()
    total = gpart[c] + gin[1 - c]
    gsend[...] = total
    gbox[f] = total

    def g_copy(k):
        return pltpu.make_async_remote_copy(
            src_ref=gsend,
            dst_ref=gbox.at[f],
            send_sem=g_send.at[k],
            recv_sem=g_recv.at[f],
            device_id={"freq": (f + k) % n_freq},
            device_id_type=MESH,
        )

    @pl.loop(1, n_freq)
    def _(k):
        g_copy(k).start()

    @pl.loop(1, n_freq)
    def _(k):
        source = (f + k) % n_freq
        pltpu.make_async_remote_copy(
            src_ref=gsend,
            dst_ref=gbox.at[source],
            send_sem=g_send.at[k],
            recv_sem=g_recv.at[source],
            device_id={"freq": source},
            device_id_type=MESH,
        ).wait_recv()

    total = jnp.sum(gbox[...], axis=0) * (1.0 / (2.0 * n_freq * SHOTS_DEV * n_freq))
    grad_ref[...] = jnp.concatenate([total[q : q + 1] for q in range(4)], axis=1)

    oper_copy(1 - c, c).wait_send()
    par_copy(c).wait_send()
    part_copy(1 - c, c).wait_send()

    @pl.loop(1, n_freq)
    def _(k):
        g_copy(k).wait_send()

    @pl.when(z == 0)
    def _():
        @pl.loop(1, n_freq)
        def _(k):
            box_copy(k).wait_send()

    @pl.loop(0, chunks)
    def _(place):
        @pl.when(z < last)
        def _():
            down_copy(place).wait_send()

        @pl.when(z > 0)
        def _():
            up_copy(place).wait_send()

        tops_here(c, place).wait()
        tops_there(1 - c, place, c).wait_send()
        tops_there(1 - c, place, 1 - c).wait_recv()


def body(traces, shot_of_trace, receiver_cell, slot_freq, operators, slowness, image_model):
    n_freq = lax.axis_size("freq")
    n_depth = lax.axis_size("depth")
    local_freqs = operators.shape[1]
    lateral = operators.shape[-1]
    shot_total = SHOTS_DEV * n_freq
    chunks = shot_total // SH
    block = (2, SH, lateral)
    vmem = pl.BlockSpec(memory_space=pltpu.VMEM)
    dma = pltpu.SemaphoreType.DMA
    gradient, tops = pl.pallas_call(
        functools.partial(kernel, n_depth, n_freq),
        out_shape=(
            jax.ShapeDtypeStruct((1, lateral), F32),
            jax.ShapeDtypeStruct((1, local_freqs, 2, shot_total, lateral), BF16),
        ),
        in_specs=[pl.BlockSpec(memory_space=pltpu.HBM)] * 7,
        out_specs=(vmem, vmem),
        scratch_shapes=[
            pltpu.SMEM(slot_freq.shape, jnp.int32),
            pltpu.VMEM(traces.shape, BF16),
            pltpu.VMEM(shot_of_trace.shape, jnp.int32),
            pltpu.VMEM(receiver_cell.shape, jnp.int32),
            pltpu.VMEM(slowness.shape, F32),
            pltpu.VMEM(image_model.shape, F32),
            pltpu.VMEM((2, 2, lateral, lateral), BF16),
            pltpu.VMEM((2, 2, lateral, lateral), BF16),
            pltpu.VMEM((2, 8, lateral), F32),
            pltpu.VMEM((2, 1, lateral), F32),
            pltpu.VMEM((2, 1, lateral), F32),
            pltpu.VMEM((n_freq, 16, 128), BF16),
            pltpu.VMEM((n_freq, 16, 128), BF16),
            pltpu.VMEM((8, SH + 32, 128), F32),
            pltpu.VMEM((chunks,) + block, BF16),
            pltpu.VMEM((chunks,) + block, BF16),
            pltpu.VMEM((2, chunks) + block, BF16),
            pltpu.VMEM((chunks,) + block, BF16),
            pltpu.VMEM((2, chunks) + block, BF16),
            pltpu.VMEM((2, 8, lateral), F32),
            pltpu.VMEM((2, 4, 128), F32),
            pltpu.VMEM((2, 4, 128), F32),
            pltpu.VMEM((4, 128), F32),
            pltpu.VMEM((n_freq, 4, 128), F32),
            dma((7,)),
            dma(()),
            dma(()),
            dma(()),
            dma(()),
            dma((n_freq,)),
            dma((n_freq,)),
            dma((chunks,)),
            dma((chunks,)),
            dma((chunks,)),
            dma((chunks,)),
            dma((chunks,)),
            dma((chunks,)),
            dma((chunks,)),
            dma(()),
            dma(()),
            dma((n_freq,)),
            dma((n_freq,)),
        ],
        compiler_params=pltpu.CompilerParams(
            collective_id=0, has_side_effects=True, vmem_limit_bytes=48 * 2**20
        ),
        cost_estimate=pl.CostEstimate(flops=2 * 10**9, bytes_accessed=4 * 10**6, transcendentals=4096),
        name="migrate",
    )(
        *[
            pltpu.with_memory_space_constraint(given, pltpu.HBM)
            for given in (slot_freq, traces, shot_of_trace, receiver_cell, slowness, image_model, operators)
        ]
    )
    return gradient, tops


def solution(mesh):
    in_specs = (
        P("freq", None),
        P("freq", None),
        P("freq", None),
        P("freq"),
        P("depth", "freq", None, None, None),
        P("depth", None),
        P("depth", None),
    )
    out_specs = (P("depth", None), P("depth", "freq", None, None, None))
    return jax.shard_map(body, mesh=mesh, in_specs=in_specs, out_specs=out_specs, check_vma=False)
```

```python
import functools

import jax
import jax.numpy as jnp
from jax import lax
from jax.experimental import pallas as pl
from jax.experimental.pallas import tpu as pltpu
from jax.sharding import PartitionSpec as P

MESH = pl.DeviceIdType.MESH
SHOTS_DEV = 6
SH = 16
F32 = jnp.float32
BF16 = jnp.bfloat16


def product(rows, matrix):
    return jnp.dot(rows, matrix, preferred_element_type=F32)


def lanes(tile, row, width):
    return jnp.concatenate([tile[4 * q + row : 4 * q + row + 1] for q in range(width // 128)], axis=1)


def kernel(
    n_depth,
    n_freq,
    slot_hbm,
    traces_hbm,
    shot_hbm,
    cell_hbm,
    slow_hbm,
    model_hbm,
    oper_ref,
    grad_ref,
    tops_ref,
    slot_ref,
    traces_ref,
    shot_ref,
    cell_ref,
    slow_ref,
    model_ref,
    opn,
    opt,
    both_down,
    both_up,
    fixed,
    par,
    cosines,
    sines,
    outbox,
    inbox,
    bins,
    din,
    dout,
    vbuf,
    uin,
    abuf,
    gacc,
    gpart,
    gin,
    gsend,
    gbox,
    load_sem,
    oper_send,
    oper_recv,
    par_send,
    par_recv,
    box_send,
    box_recv,
    down_send,
    down_recv,
    up_send,
    up_recv,
    tops_local,
    tops_send,
    tops_recv,
    part_send,
    part_recv,
    g_send,
    g_recv,
):
    d = lax.axis_index("depth")
    f = lax.axis_index("freq")
    z = d // 2
    c = d % 2
    chunks = din.shape[0]
    lateral = din.shape[-1]
    last = n_depth // 2 - 1
    base = 2 * z
    partner = base + 1 - c

    def at(depth):
        return {"depth": depth}

    first_chunk = (f * SHOTS_DEV) // SH

    def chunk_of(place):
        return (first_chunk + place) % chunks

    below = (d + 2) % n_depth
    above = (d + n_depth - 2) % n_depth

    barrier = pltpu.get_barrier_semaphore()

    def greet(depth):
        pl.semaphore_signal(barrier, inc=1, device_id=at(depth), device_id_type=MESH)

    def greet_group(k):
        pl.semaphore_signal(barrier, inc=1, device_id={"freq": (f + k) % n_freq}, device_id_type=MESH)

    greet_group(n_freq // 2)

    @pl.loop(1, n_freq // 2)
    def _(k):
        greet_group(n_freq // 2 + k)
        greet_group(n_freq // 2 - k)

    greet(partner)

    @pl.when(z > 0)
    def _():
        greet(above)

    @pl.when(z < last)
    def _():
        greet(below)

    greeted = n_freq + jnp.where(z > 0, 1, 0) + jnp.where(z < last, 1, 0)

    loads = [
        pltpu.make_async_copy(source, target, load_sem.at[i])
        for i, (source, target) in enumerate(
            [
                (slow_hbm, slow_ref),
                (model_hbm, model_ref),
                (slot_hbm, slot_ref),
                (traces_hbm, traces_ref),
                (shot_hbm, shot_ref),
                (cell_hbm, cell_ref),
                (oper_ref.at[0, c], opn.at[c]),
            ]
        )
    ]

    @pl.when(z == 0)
    def _():
        for load in loads[3:6]:
            load.start()

    for load in loads[:3] + loads[6:]:
        load.start()
    for load in loads[:2]:
        load.wait()

    row8 = lax.broadcasted_iota(jnp.int32, (8, lateral), 0)
    par[c] = jnp.where(row8 == 0, slow_ref[...], model_ref[...])

    @pl.when(z == 0)
    def _():
        for load in loads[3:6]:
            load.wait()
        rows = n_freq * 16
        row = lax.broadcasted_iota(jnp.int32, (rows, 128), 0)
        column = lax.broadcasted_iota(jnp.int32, (rows, 128), 1)
        group, within = row // 16, row % 16
        kind, piece = within % 4, within // 4
        wanted = jnp.where(kind < 2, group * 4 + 2 * c + kind, -1)
        total = jnp.zeros((rows, 128), F32)
        for q in range(4):
            select = jnp.where((column == wanted) & (piece == q), 1.0, 0.0).astype(BF16)
            total += lax.dot_general(
                select,
                traces_ref[128 * q : 128 * (q + 1), :],
                (((1,), (1,)), ((), ())),
                preferred_element_type=F32,
            )
        cell = cell_ref[...]
        first = (cell // 128 * 8 + shot_ref[...]).astype(F32)
        second = (cell % 128).astype(F32)
        row16 = lax.broadcasted_iota(jnp.int32, (16, 128), 0)
        label = jnp.zeros((16, 128), F32)
        for q in range(4):
            label = jnp.where(row16 == 4 * q + 2, first[:, 128 * q : 128 * (q + 1)], label)
            label = jnp.where(row16 == 4 * q + 3, second[:, 128 * q : 128 * (q + 1)], label)
        filled = total.reshape(n_freq, 16, 128) + label[None]
        outbox[...] = filled.astype(BF16)
        inbox[f] = outbox[f]

    pl.semaphore_wait(barrier, greeted)

    def box_copy(k):
        return pltpu.make_async_remote_copy(
            src_ref=outbox.at[(f + k) % n_freq],
            dst_ref=inbox.at[f],
            send_sem=box_send.at[k],
            recv_sem=box_recv.at[f],
            device_id={"freq": (f + k) % n_freq},
            device_id_type=MESH,
        )

    @pl.when(z == 0)
    def _():
        @pl.loop(1, n_freq // 2)
        def _(k):
            box_copy(k).start()
            box_copy(n_freq - k).start()

        box_copy(n_freq // 2).start()

    def par_copy(index):
        return pltpu.make_async_remote_copy(
            src_ref=par.at[index],
            dst_ref=par.at[index],
            send_sem=par_send,
            recv_sem=par_recv,
            device_id=at(partner),
            device_id_type=MESH,
        )

    def oper_copy(slot, index):
        return pltpu.make_async_remote_copy(
            src_ref=oper_ref.at[0, slot],
            dst_ref=opn.at[index],
            send_sem=oper_send,
            recv_sem=oper_recv,
            device_id=at(partner),
            device_id_type=MESH,
        )

    oper_copy(1 - c, c).start()
    par_copy(c).start()

    loads[2].wait()
    loads[6].wait()
    scale = 0.1 * (slot_ref[c].astype(F32) + 1.0)

    def angles(e):
        theta = scale * par[e, 0:1, :]
        cosines[e] = jnp.cos(theta)
        sines[e] = jnp.sin(theta)

    gacc[...] = jnp.zeros_like(gacc)
    for p in range(2):
        opt[c, p] = opn[c, p].T
    par_copy(1 - c).wait_recv()
    angles(0)
    angles(1)
    oper_copy(c, 1 - c).wait_recv()

    for p in range(2):
        opt[1 - c, p] = opn[1 - c, p].T

    def wait_box(source):
        @pl.when(source != f)
        def _():
            pltpu.make_async_remote_copy(
                src_ref=outbox.at[source],
                dst_ref=inbox.at[source],
                send_sem=box_send.at[source],
                recv_sem=box_recv.at[source],
                device_id={"freq": source},
                device_id_type=MESH,
            ).wait_recv()

    counts = [(SH * j + SH - 1) // SHOTS_DEV - SH * j // SHOTS_DEV + 1 for j in range(chunks)]
    fewest, most = min(counts), max(counts)

    def bin_chunk(place):
        j = chunk_of(place)
        start = SH * j
        first_source = start // SHOTS_DEV
        fresh = jnp.where(place == 0, first_source, (start + SHOTS_DEV - 1) // SHOTS_DEV)
        after = jnp.where(
            (place == chunks - 1) & (first_chunk > 0),
            (SH * first_chunk) // SHOTS_DEV,
            (start + SH - 1) // SHOTS_DEV + 1,
        )

        @pl.loop(fresh, after)
        def _(source):
            wait_box(source)

        top = 8 + SHOTS_DEV * first_source - start
        row = lax.broadcasted_iota(jnp.int32, (32, 4 * 128), 0).astype(F32)
        lane_row = lax.broadcasted_iota(jnp.int32, (128, 4 * 128), 0).astype(F32)

        def add_source(i):
            tile = inbox[first_source + i].astype(F32)
            real, imag = lanes(tile, 0, 512), lanes(tile, 1, 512)
            first, low = lanes(tile, 2, 512), lanes(tile, 3, 512)
            hit = row == first
            left = jnp.concatenate(
                [jnp.where(hit, real, 0.0).astype(BF16), jnp.where(hit, imag, 0.0).astype(BF16)], axis=0
            )
            right = jnp.where(lane_row == low, 1.0, 0.0).astype(BF16)
            part = lax.dot_general(left, right, (((1,), (1,)), ((), ())), preferred_element_type=F32)
            for g in range(8):
                bins[g, pl.ds(top + SHOTS_DEV * i, 8), :] = part[8 * g : 8 * (g + 1)]

        for i in range(fewest):
            add_source(i)

        for i in range(fewest, most):

            @pl.when(first_source + i <= (start + SH - 1) // SHOTS_DEV)
            def _():
                add_source(i)

        for p in range(2):
            for high in range(4):
                din[place, p, :, 128 * high : 128 * (high + 1)] = bins[4 * p + high, 8 : 8 + SH, :].astype(BF16)

    def down_copy(place):
        return pltpu.make_async_remote_copy(
            src_ref=dout.at[place],
            dst_ref=din.at[place],
            send_sem=down_send.at[place],
            recv_sem=down_recv.at[place],
            device_id=at(below),
            device_id_type=MESH,
        )

    def up_copy(place):
        return pltpu.make_async_remote_copy(
            src_ref=abuf.at[0, place],
            dst_ref=uin.at[place],
            send_sem=up_send.at[place],
            recv_sem=up_recv.at[place],
            device_id=at(above),
            device_id_type=MESH,
        )

    def load(ref, place, n):
        return [ref[pl.ds(place, n), p].reshape(n * SH, lateral).astype(F32) for p in range(2)]

    def store(ref, place, n, real, imag):
        ref[pl.ds(place, n), 0] = real.reshape(n, SH, lateral)
        ref[pl.ds(place, n), 1] = imag.reshape(n, SH, lateral)

    def shift(e, place, n, real, imag):
        cos_row, sin_row = cosines[e], sines[e]
        shifted_real = (cos_row * real - sin_row * imag).astype(BF16)
        shifted_imag = (cos_row * imag + sin_row * real).astype(BF16)
        store(vbuf.at[e], place, n, shifted_real, shifted_imag)
        return jnp.concatenate([shifted_real, shifted_imag], axis=0)

    def forward(table, stacked):
        rows = stacked.shape[0] // 2
        by_real, by_imag = product(stacked, table[0]), product(stacked, table[1])
        return (by_real[:rows] - by_imag[rows:]).astype(BF16), (by_imag[:rows] + by_real[rows:]).astype(BF16)

    def down(place, n, send):
        stacked = shift(0, place, n, *load(din, place, n))
        real, imag = forward(opt.at[0], stacked)
        stacked = shift(1, place, n, real.astype(F32), imag.astype(F32))
        if send:
            real, imag = forward(opt.at[1], stacked)
            store(dout, place, n, real, imag)
            for i in range(n):
                down_copy(place + i).start()

    def down_inner(place):
        stacked = shift(0, place, 1, *load(din, place, 1))
        real, imag = forward(both_down, stacked)
        store(dout, place, 1, real, imag)
        down_copy(place).start()
        real, imag = forward(opt.at[0], stacked)
        shift(1, place, 1, real.astype(F32), imag.astype(F32))

    def rows_of(place):
        return pl.ds(pl.multiple_of(chunk_of(place) * SH, SH), SH)

    def tops_here(e, place):
        return pltpu.make_async_copy(abuf.at[e, place], tops_ref.at[0, c, :, rows_of(place), :], tops_local.at[place])

    def tops_there(e, place, its_slot):
        return pltpu.make_async_remote_copy(
            src_ref=abuf.at[e, place],
            dst_ref=tops_ref.at[0, its_slot, :, rows_of(place), :],
            send_sem=tops_send.at[place],
            recv_sem=tops_recv.at[place],
            device_id=at(partner),
            device_id_type=MESH,
        )

    def back(table, e, real, imag):
        rows = real.shape[0]
        stacked = jnp.concatenate([real.astype(BF16), imag.astype(BF16)], axis=0)
        by_real, by_imag = product(stacked, table[0]), product(stacked, table[1])
        back_real = by_real[:rows] + by_imag[rows:]
        back_imag = by_real[rows:] - by_imag[:rows]
        cos_row, sin_row = cosines[e], sines[e]
        return cos_row * back_real + sin_row * back_imag, cos_row * back_imag - sin_row * back_real

    def source_of(e, place, n, real, imag):
        old_real, old_imag = load(vbuf.at[e], place, n)
        model = par[e, 1:2, :]
        source_real = real + model * old_real
        source_imag = imag + model * old_imag
        term = old_real * source_real + old_imag * source_imag
        gacc[e] += jnp.sum(term.reshape(n * SH // 8, 8, lateral), axis=0)
        return source_real, source_imag

    def finish(e, place, n, real, imag):
        real, imag = real.astype(BF16), imag.astype(BF16)
        store(abuf.at[e], place, n, real, imag)
        for i in range(n):
            if e == 0:

                @pl.when(z > 0)
                def _():
                    up_copy(place + i).start()

            @pl.when(c == e)
            def _():
                tops_here(e, place + i).start()

            @pl.when(c != e)
            def _():
                tops_there(e, place + i, c).start()

        return real.astype(F32), imag.astype(F32)

    def backward(e, place, n, real, imag):
        return finish(e, place, n, *back(opn.at[e], e, *source_of(e, place, n, real, imag)))

    def prepare(place):
        old_real, old_imag = load(vbuf.at[0], place, 1)
        model = par[0, 1:2, :]
        store(fixed, place, 1, *back(opn.at[0], 0, model * old_real, model * old_imag))

    def up_inner(place):
        real, imag = source_of(1, place, 1, *load(uin, place, 1))
        fixed_real, fixed_imag = load(fixed, place, 1)
        top_real, top_imag = back(both_up, 0, real, imag)
        finish(0, place, 1, top_real + fixed_real, top_imag + fixed_imag)
        source_of(0, place, 1, *finish(1, place, 1, *back(opn.at[1], 1, real, imag)))

    def up(place, n, real, imag):
        real, imag = backward(1, place, n, real, imag)
        backward(0, place, n, real, imag)

    @pl.when(z == 0)
    def _():
        bin_chunk(0)
        down(0, 1, True)

        @pl.loop(0, (chunks - 2) // 2)
        def _(turn):
            place = 1 + 2 * turn
            bin_chunk(place)
            bin_chunk(place + 1)
            down(place, 2, True)

        bin_chunk(chunks - 1)
        down(chunks - 1, 1, True)

    @pl.when((z > 0) & (z < last))
    def _():
        @pl.loop(0, lateral // 64)
        def _(block):
            rows = pl.ds(pl.multiple_of(block * 64, 64), 64)
            real, imag = opt[0, 0, rows, :].astype(F32), opt[0, 1, rows, :].astype(F32)
            cos_row, sin_row = cosines[1], sines[1]
            stacked = jnp.concatenate(
                [(cos_row * real - sin_row * imag).astype(BF16), (cos_row * imag + sin_row * real).astype(BF16)],
                axis=0,
            )
            both_down[0, rows, :], both_down[1, rows, :] = forward(opt.at[1], stacked)

        for p in range(2):
            both_up[p] = both_down[p].T

        @pl.loop(0, chunks)
        def _(place):
            down_copy(place).wait_recv()
            down_inner(place)

    @pl.when(z == last)
    def _():
        def turn_round(place, n):
            for i in range(n):
                down_copy(place + i).wait_recv()
            down(place, n, False)
            nothing = jnp.zeros((n * SH, lateral), F32)
            up(place, n, nothing, nothing)

        @pl.loop(0, (chunks - 2) // 2)
        def _(turn):
            turn_round(2 * turn, 2)

        @pl.loop(chunks - 2, chunks)
        def _(place):
            turn_round(place, 1)

    inner = (z > 0) & (z < last - 1)

    @pl.when(inner)
    def _():
        @pl.loop(0, chunks)
        def _(place):
            prepare(place)

        @pl.loop(0, chunks)
        def _(place):
            up_copy(place).wait_recv()
            up_inner(place)

    @pl.when((z == 0) | (z == last - 1))
    def _():
        @pl.loop(0, chunks)
        def _(place):
            up_copy(place).wait_recv()
            up(place, 1, *load(uin, place, 1))

    row4 = lax.broadcasted_iota(jnp.int32, (4, 128), 0)

    def rows_tile(summed):
        tile = jnp.zeros((4, 128), F32)
        for q in range(4):
            tile = jnp.where(row4 == q, summed[:, 128 * q : 128 * (q + 1)], tile)
        return tile

    def part_copy(e, sender):
        return pltpu.make_async_remote_copy(
            src_ref=gpart.at[e],
            dst_ref=gin.at[sender],
            send_sem=part_send,
            recv_sem=part_recv,
            device_id=at(partner),
            device_id_type=MESH,
        )

    for e in range(2):
        gpart[e] = rows_tile(jnp.sum(gacc[e], axis=0, keepdims=True))

        @pl.when(c != e)
        def _():
            part_copy(e, c).start()

    part_copy(0, 1 - c).wait_recv()
    total = gpart[c] + gin[1 - c]
    gsend[...] = total
    gbox[f] = total

    def g_copy(k):
        return pltpu.make_async_remote_copy(
            src_ref=gsend,
            dst_ref=gbox.at[f],
            send_sem=g_send.at[k],
            recv_sem=g_recv.at[f],
            device_id={"freq": (f + k) % n_freq},
            device_id_type=MESH,
        )

    @pl.loop(1, n_freq)
    def _(k):
        g_copy(k).start()

    @pl.loop(1, n_freq)
    def _(k):
        source = (f + k) % n_freq
        pltpu.make_async_remote_copy(
            src_ref=gsend,
            dst_ref=gbox.at[source],
            send_sem=g_send.at[k],
            recv_sem=g_recv.at[source],
            device_id={"freq": source},
            device_id_type=MESH,
        ).wait_recv()

    total = jnp.sum(gbox[...], axis=0) * (1.0 / (2.0 * n_freq * SHOTS_DEV * n_freq))
    grad_ref[...] = jnp.concatenate([total[q : q + 1] for q in range(4)], axis=1)

    oper_copy(1 - c, c).wait_send()
    par_copy(c).wait_send()
    part_copy(1 - c, c).wait_send()

    @pl.loop(1, n_freq)
    def _(k):
        g_copy(k).wait_send()

    @pl.when(z == 0)
    def _():
        @pl.loop(1, n_freq)
        def _(k):
            box_copy(k).wait_send()

    @pl.loop(0, chunks)
    def _(place):
        @pl.when(z < last)
        def _():
            down_copy(place).wait_send()

        @pl.when(z > 0)
        def _():
            up_copy(place).wait_send()

        tops_here(c, place).wait()
        tops_there(1 - c, place, c).wait_send()
        tops_there(1 - c, place, 1 - c).wait_recv()


def body(traces, shot_of_trace, receiver_cell, slot_freq, operators, slowness, image_model):
    n_freq = lax.axis_size("freq")
    n_depth = lax.axis_size("depth")
    local_freqs = operators.shape[1]
    lateral = operators.shape[-1]
    shot_total = SHOTS_DEV * n_freq
    chunks = shot_total // SH
    block = (2, SH, lateral)
    vmem = pl.BlockSpec(memory_space=pltpu.VMEM)
    dma = pltpu.SemaphoreType.DMA
    gradient, tops = pl.pallas_call(
        functools.partial(kernel, n_depth, n_freq),
        out_shape=(
            jax.ShapeDtypeStruct((1, lateral), F32),
            jax.ShapeDtypeStruct((1, local_freqs, 2, shot_total, lateral), BF16),
        ),
        in_specs=[pl.BlockSpec(memory_space=pltpu.HBM)] * 7,
        out_specs=(vmem, vmem),
        scratch_shapes=[
            pltpu.SMEM(slot_freq.shape, jnp.int32),
            pltpu.VMEM(traces.shape, BF16),
            pltpu.VMEM(shot_of_trace.shape, jnp.int32),
            pltpu.VMEM(receiver_cell.shape, jnp.int32),
            pltpu.VMEM(slowness.shape, F32),
            pltpu.VMEM(image_model.shape, F32),
            pltpu.VMEM((2, 2, lateral, lateral), BF16),
            pltpu.VMEM((2, 2, lateral, lateral), BF16),
            pltpu.VMEM((2, lateral, lateral), BF16),
            pltpu.VMEM((2, lateral, lateral), BF16),
            pltpu.VMEM((chunks,) + block, F32),
            pltpu.VMEM((2, 8, lateral), F32),
            pltpu.VMEM((2, 1, lateral), F32),
            pltpu.VMEM((2, 1, lateral), F32),
            pltpu.VMEM((n_freq, 16, 128), BF16),
            pltpu.VMEM((n_freq, 16, 128), BF16),
            pltpu.VMEM((8, SH + 32, 128), F32),
            pltpu.VMEM((chunks,) + block, BF16),
            pltpu.VMEM((chunks,) + block, BF16),
            pltpu.VMEM((2, chunks) + block, BF16),
            pltpu.VMEM((chunks,) + block, BF16),
            pltpu.VMEM((2, chunks) + block, BF16),
            pltpu.VMEM((2, 8, lateral), F32),
            pltpu.VMEM((2, 4, 128), F32),
            pltpu.VMEM((2, 4, 128), F32),
            pltpu.VMEM((4, 128), F32),
            pltpu.VMEM((n_freq, 4, 128), F32),
            dma((7,)),
            dma(()),
            dma(()),
            dma(()),
            dma(()),
            dma((n_freq,)),
            dma((n_freq,)),
            dma((chunks,)),
            dma((chunks,)),
            dma((chunks,)),
            dma((chunks,)),
            dma((chunks,)),
            dma((chunks,)),
            dma((chunks,)),
            dma(()),
            dma(()),
            dma((n_freq,)),
            dma((n_freq,)),
        ],
        compiler_params=pltpu.CompilerParams(
            collective_id=0, has_side_effects=True, vmem_limit_bytes=48 * 2**20
        ),
        cost_estimate=pl.CostEstimate(flops=2 * 10**9, bytes_accessed=4 * 10**6, transcendentals=4096),
        name="migrate",
    )(
        *[
            pltpu.with_memory_space_constraint(given, pltpu.HBM)
            for given in (slot_freq, traces, shot_of_trace, receiver_cell, slowness, image_model, operators)
        ]
    )
    return gradient, tops


def solution(mesh):
    in_specs = (
        P("freq", None),
        P("freq", None),
        P("freq", None),
        P("freq"),
        P("depth", "freq", None, None, None),
        P("depth", None),
        P("depth", None),
    )
    out_specs = (P("depth", None), P("depth", "freq", None, None, None))
    return jax.shard_map(body, mesh=mesh, in_specs=in_specs, out_specs=out_specs, check_vma=False)
```

```python
import functools

import jax
import jax.numpy as jnp
from jax import lax
from jax.experimental import pallas as pl
from jax.experimental.pallas import tpu as pltpu
from jax.sharding import PartitionSpec as P

MESH = pl.DeviceIdType.MESH
SHOTS_DEV = 6
SH = 16
F32 = jnp.float32
BF16 = jnp.bfloat16


def product(rows, matrix):
    return jnp.dot(rows, matrix, preferred_element_type=F32)


def lanes(tile, row, width):
    return jnp.concatenate([tile[4 * q + row : 4 * q + row + 1] for q in range(width // 128)], axis=1)


def kernel(
    n_depth,
    n_freq,
    slot_hbm,
    traces_hbm,
    shot_hbm,
    cell_hbm,
    slow_hbm,
    model_hbm,
    oper_ref,
    grad_ref,
    tops_ref,
    slot_ref,
    traces_ref,
    shot_ref,
    cell_ref,
    slow_ref,
    model_ref,
    opn,
    opt,
    both_down,
    both_up,
    fixed,
    par,
    cosines,
    sines,
    outbox,
    inbox,
    bins,
    din,
    dout,
    vbuf,
    uin,
    abuf,
    gacc,
    gpart,
    gin,
    gsend,
    gbox,
    load_sem,
    oper_send,
    oper_recv,
    par_send,
    par_recv,
    box_send,
    box_recv,
    down_send,
    down_recv,
    up_send,
    up_recv,
    tops_local,
    tops_send,
    tops_recv,
    part_send,
    part_recv,
    g_send,
    g_recv,
):
    d = lax.axis_index("depth")
    f = lax.axis_index("freq")
    z = d // 2
    c = d % 2
    chunks = din.shape[0]
    lateral = din.shape[-1]
    last = n_depth // 2 - 1
    base = 2 * z
    partner = base + 1 - c

    def at(depth):
        return {"depth": depth}

    first_chunk = (f * SHOTS_DEV) // SH

    def chunk_of(place):
        return (first_chunk + place) % chunks

    below = (d + 2) % n_depth
    above = (d + n_depth - 2) % n_depth

    barrier = pltpu.get_barrier_semaphore()

    def greet(depth):
        pl.semaphore_signal(barrier, inc=1, device_id=at(depth), device_id_type=MESH)

    def greet_group(k):
        pl.semaphore_signal(barrier, inc=1, device_id={"freq": (f + k) % n_freq}, device_id_type=MESH)

    greet_group(n_freq // 2)

    @pl.loop(1, n_freq // 2)
    def _(k):
        greet_group(n_freq // 2 + k)
        greet_group(n_freq // 2 - k)

    greet(partner)

    @pl.when(z > 0)
    def _():
        greet(above)

    @pl.when(z < last)
    def _():
        greet(below)

    greeted = n_freq + jnp.where(z > 0, 1, 0) + jnp.where(z < last, 1, 0)

    loads = [
        pltpu.make_async_copy(source, target, load_sem.at[i])
        for i, (source, target) in enumerate(
            [
                (slow_hbm, slow_ref),
                (model_hbm, model_ref),
                (slot_hbm, slot_ref),
                (traces_hbm, traces_ref),
                (shot_hbm, shot_ref),
                (cell_hbm, cell_ref),
                (oper_ref.at[0, c], opn.at[c]),
            ]
        )
    ]

    @pl.when(z == 0)
    def _():
        for load in loads[3:6]:
            load.start()

    for load in loads[:3] + loads[6:]:
        load.start()
    for load in loads[:2]:
        load.wait()

    row8 = lax.broadcasted_iota(jnp.int32, (8, lateral), 0)
    par[c] = jnp.where(row8 == 0, slow_ref[...], model_ref[...])

    @pl.when(z == 0)
    def _():
        for load in loads[3:6]:
            load.wait()
        rows = n_freq * 16
        row = lax.broadcasted_iota(jnp.int32, (rows, 128), 0)
        column = lax.broadcasted_iota(jnp.int32, (rows, 128), 1)
        group, within = row // 16, row % 16
        kind, piece = within % 4, within // 4
        wanted = jnp.where(kind < 2, group * 4 + 2 * c + kind, -1)
        total = jnp.zeros((rows, 128), F32)
        for q in range(4):
            select = jnp.where((column == wanted) & (piece == q), 1.0, 0.0).astype(BF16)
            total += lax.dot_general(
                select,
                traces_ref[128 * q : 128 * (q + 1), :],
                (((1,), (1,)), ((), ())),
                preferred_element_type=F32,
            )
        cell = cell_ref[...]
        first = (cell // 128 * 8 + shot_ref[...]).astype(F32)
        second = (cell % 128).astype(F32)
        row16 = lax.broadcasted_iota(jnp.int32, (16, 128), 0)
        label = jnp.zeros((16, 128), F32)
        for q in range(4):
            label = jnp.where(row16 == 4 * q + 2, first[:, 128 * q : 128 * (q + 1)], label)
            label = jnp.where(row16 == 4 * q + 3, second[:, 128 * q : 128 * (q + 1)], label)
        filled = total.reshape(n_freq, 16, 128) + label[None]
        outbox[...] = filled.astype(BF16)
        inbox[f] = outbox[f]

    pl.semaphore_wait(barrier, greeted)

    def box_copy(k):
        return pltpu.make_async_remote_copy(
            src_ref=outbox.at[(f + k) % n_freq],
            dst_ref=inbox.at[f],
            send_sem=box_send.at[k],
            recv_sem=box_recv.at[f],
            device_id={"freq": (f + k) % n_freq},
            device_id_type=MESH,
        )

    @pl.when(z == 0)
    def _():
        @pl.loop(1, n_freq // 2)
        def _(k):
            box_copy(k).start()
            box_copy(n_freq - k).start()

        box_copy(n_freq // 2).start()

    def par_copy(index):
        return pltpu.make_async_remote_copy(
            src_ref=par.at[index],
            dst_ref=par.at[index],
            send_sem=par_send,
            recv_sem=par_recv,
            device_id=at(partner),
            device_id_type=MESH,
        )

    def oper_copy(slot, index):
        return pltpu.make_async_remote_copy(
            src_ref=oper_ref.at[0, slot],
            dst_ref=opn.at[index],
            send_sem=oper_send,
            recv_sem=oper_recv,
            device_id=at(partner),
            device_id_type=MESH,
        )

    oper_copy(1 - c, c).start()
    par_copy(c).start()

    loads[2].wait()
    loads[6].wait()
    scale = 0.1 * (slot_ref[c].astype(F32) + 1.0)

    def angles(e):
        theta = scale * par[e, 0:1, :]
        cosines[e] = jnp.cos(theta)
        sines[e] = jnp.sin(theta)

    gacc[...] = jnp.zeros_like(gacc)
    for p in range(2):
        opt[c, p] = opn[c, p].T
    par_copy(1 - c).wait_recv()
    angles(0)
    angles(1)
    oper_copy(c, 1 - c).wait_recv()

    for p in range(2):
        opt[1 - c, p] = opn[1 - c, p].T

    def wait_box(source):
        @pl.when(source != f)
        def _():
            pltpu.make_async_remote_copy(
                src_ref=outbox.at[source],
                dst_ref=inbox.at[source],
                send_sem=box_send.at[source],
                recv_sem=box_recv.at[source],
                device_id={"freq": source},
                device_id_type=MESH,
            ).wait_recv()

    counts = [(SH * j + SH - 1) // SHOTS_DEV - SH * j // SHOTS_DEV + 1 for j in range(chunks)]
    fewest, most = min(counts), max(counts)

    def bin_chunk(place):
        j = chunk_of(place)
        start = SH * j
        first_source = start // SHOTS_DEV
        fresh = jnp.where(place == 0, first_source, (start + SHOTS_DEV - 1) // SHOTS_DEV)
        after = jnp.where(
            (place == chunks - 1) & (first_chunk > 0),
            (SH * first_chunk) // SHOTS_DEV,
            (start + SH - 1) // SHOTS_DEV + 1,
        )

        @pl.loop(fresh, after)
        def _(source):
            wait_box(source)

        top = 8 + SHOTS_DEV * first_source - start
        row = lax.broadcasted_iota(jnp.int32, (32, 4 * 128), 0).astype(F32)
        lane_row = lax.broadcasted_iota(jnp.int32, (128, 4 * 128), 0).astype(F32)

        def add_source(i):
            tile = inbox[first_source + i].astype(F32)
            real, imag = lanes(tile, 0, 512), lanes(tile, 1, 512)
            first, low = lanes(tile, 2, 512), lanes(tile, 3, 512)
            hit = row == first
            left = jnp.concatenate(
                [jnp.where(hit, real, 0.0).astype(BF16), jnp.where(hit, imag, 0.0).astype(BF16)], axis=0
            )
            right = jnp.where(lane_row == low, 1.0, 0.0).astype(BF16)
            part = lax.dot_general(left, right, (((1,), (1,)), ((), ())), preferred_element_type=F32)
            for g in range(8):
                bins[g, pl.ds(top + SHOTS_DEV * i, 8), :] = part[8 * g : 8 * (g + 1)]

        for i in range(fewest):
            add_source(i)

        for i in range(fewest, most):

            @pl.when(first_source + i <= (start + SH - 1) // SHOTS_DEV)
            def _():
                add_source(i)

        for p in range(2):
            for high in range(4):
                din[place, p, :, 128 * high : 128 * (high + 1)] = bins[4 * p + high, 8 : 8 + SH, :].astype(BF16)

    def down_copy(place):
        return pltpu.make_async_remote_copy(
            src_ref=dout.at[place],
            dst_ref=din.at[place],
            send_sem=down_send.at[place],
            recv_sem=down_recv.at[place],
            device_id=at(below),
            device_id_type=MESH,
        )

    def up_copy(place):
        return pltpu.make_async_remote_copy(
            src_ref=abuf.at[0, place],
            dst_ref=uin.at[place],
            send_sem=up_send.at[place],
            recv_sem=up_recv.at[place],
            device_id=at(above),
            device_id_type=MESH,
        )

    def load(ref, place, n):
        return [ref[pl.ds(place, n), p].reshape(n * SH, lateral).astype(F32) for p in range(2)]

    def store(ref, place, n, real, imag):
        ref[pl.ds(place, n), 0] = real.reshape(n, SH, lateral)
        ref[pl.ds(place, n), 1] = imag.reshape(n, SH, lateral)

    def shift(e, place, n, real, imag):
        cos_row, sin_row = cosines[e], sines[e]
        shifted_real = (cos_row * real - sin_row * imag).astype(BF16)
        shifted_imag = (cos_row * imag + sin_row * real).astype(BF16)
        store(vbuf.at[e], place, n, shifted_real, shifted_imag)
        return jnp.concatenate([shifted_real, shifted_imag], axis=0)

    def forward(table, stacked):
        rows = stacked.shape[0] // 2
        by_real, by_imag = product(stacked, table[0]), product(stacked, table[1])
        return (by_real[:rows] - by_imag[rows:]).astype(BF16), (by_imag[:rows] + by_real[rows:]).astype(BF16)

    def down(place, n):
        stacked = shift(0, place, n, *load(din, place, n))
        real, imag = forward(opt.at[0], stacked)
        stacked = shift(1, place, n, real.astype(F32), imag.astype(F32))
        real, imag = forward(opt.at[1], stacked)
        store(dout, place, n, real, imag)
        for i in range(n):
            down_copy(place + i).start()

    def down_first(place):
        down_copy(place).wait_recv()
        stacked = shift(0, place, 1, *load(din, place, 1))
        store(dout, place, 1, *forward(both_down, stacked))
        down_copy(place).start()

    def second_step(place, n):
        stacked = jnp.concatenate([part.astype(BF16) for part in load(vbuf.at[0], place, n)], axis=0)
        real, imag = forward(opt.at[0], stacked)
        shift(1, place, n, real.astype(F32), imag.astype(F32))

    def rows_of(place):
        return pl.ds(pl.multiple_of(chunk_of(place) * SH, SH), SH)

    def tops_here(e, place):
        return pltpu.make_async_copy(abuf.at[e, place], tops_ref.at[0, c, :, rows_of(place), :], tops_local.at[place])

    def tops_there(e, place, its_slot):
        return pltpu.make_async_remote_copy(
            src_ref=abuf.at[e, place],
            dst_ref=tops_ref.at[0, its_slot, :, rows_of(place), :],
            send_sem=tops_send.at[place],
            recv_sem=tops_recv.at[place],
            device_id=at(partner),
            device_id_type=MESH,
        )

    def back(table, e, real, imag):
        rows = real.shape[0]
        stacked = jnp.concatenate([real.astype(BF16), imag.astype(BF16)], axis=0)
        by_real, by_imag = product(stacked, table[0]), product(stacked, table[1])
        back_real = by_real[:rows] + by_imag[rows:]
        back_imag = by_real[rows:] - by_imag[:rows]
        cos_row, sin_row = cosines[e], sines[e]
        return cos_row * back_real + sin_row * back_imag, cos_row * back_imag - sin_row * back_real

    def source_of(e, place, n, real, imag):
        old_real, old_imag = load(vbuf.at[e], place, n)
        model = par[e, 1:2, :]
        source_real = real + model * old_real
        source_imag = imag + model * old_imag
        term = old_real * source_real + old_imag * source_imag
        gacc[e] += jnp.sum(term.reshape(n * SH // 8, 8, lateral), axis=0)
        return source_real, source_imag

    def finish(e, place, n, real, imag):
        real, imag = real.astype(BF16), imag.astype(BF16)
        store(abuf.at[e], place, n, real, imag)
        for i in range(n):
            if e == 0:

                @pl.when(z > 0)
                def _():
                    up_copy(place + i).start()

            @pl.when(c == e)
            def _():
                tops_here(e, place + i).start()

            @pl.when(c != e)
            def _():
                tops_there(e, place + i, c).start()

        return real.astype(F32), imag.astype(F32)

    def backward(e, place, n, real, imag):
        return finish(e, place, n, *back(opn.at[e], e, *source_of(e, place, n, real, imag)))

    def prepare(place, n):
        old_real, old_imag = load(vbuf.at[0], place, n)
        model = par[0, 1:2, :]
        store(fixed, place, n, *back(opn.at[0], 0, model * old_real, model * old_imag))

    def up_first(place):
        up_copy(place).wait_recv()
        real, imag = source_of(1, place, 1, *load(uin, place, 1))
        store(uin, place, 1, real.astype(BF16), imag.astype(BF16))
        fixed_real, fixed_imag = load(fixed, place, 1)
        top_real, top_imag = back(both_up, 0, real, imag)
        finish(0, place, 1, top_real + fixed_real, top_imag + fixed_imag)

    def up_rest(place, n):
        source_of(0, place, n, *finish(1, place, n, *back(opn.at[1], 1, *load(uin, place, n))))

    def up(place, n, real, imag):
        real, imag = backward(1, place, n, real, imag)
        backward(0, place, n, real, imag)

    row4 = lax.broadcasted_iota(jnp.int32, (4, 128), 0)

    def rows_tile(summed):
        tile = jnp.zeros((4, 128), F32)
        for q in range(4):
            tile = jnp.where(row4 == q, summed[:, 128 * q : 128 * (q + 1)], tile)
        return tile

    def part_copy(e, sender):
        return pltpu.make_async_remote_copy(
            src_ref=gpart.at[e],
            dst_ref=gin.at[sender],
            send_sem=part_send,
            recv_sem=part_recv,
            device_id=at(partner),
            device_id_type=MESH,
        )

    def g_copy(k):
        return pltpu.make_async_remote_copy(
            src_ref=gsend,
            dst_ref=gbox.at[f],
            send_sem=g_send.at[k],
            recv_sem=g_recv.at[f],
            device_id={"freq": (f + k) % n_freq},
            device_id_type=MESH,
        )

    def share_gradient():
        for e in range(2):
            gpart[e] = rows_tile(jnp.sum(gacc[e], axis=0, keepdims=True))

            @pl.when(c != e)
            def _():
                part_copy(e, c).start()

        part_copy(0, 1 - c).wait_recv()
        total = gpart[c] + gin[1 - c]
        gsend[...] = total
        gbox[f] = total

        @pl.loop(1, n_freq)
        def _(k):
            g_copy(k).start()

    @pl.when(z == 0)
    def _():
        bin_chunk(0)
        down(0, 1)

        @pl.loop(0, (chunks - 2) // 2)
        def _(turn):
            place = 1 + 2 * turn
            bin_chunk(place)
            bin_chunk(place + 1)
            down(place, 2)

        bin_chunk(chunks - 1)
        down(chunks - 1, 1)

    @pl.when((z > 0) & (z < last))
    def _():
        @pl.loop(0, lateral // 64)
        def _(block):
            rows = pl.ds(pl.multiple_of(block * 64, 64), 64)
            real, imag = opt[0, 0, rows, :].astype(F32), opt[0, 1, rows, :].astype(F32)
            cos_row, sin_row = cosines[1], sines[1]
            stacked = jnp.concatenate(
                [(cos_row * real - sin_row * imag).astype(BF16), (cos_row * imag + sin_row * real).astype(BF16)],
                axis=0,
            )
            both_down[0, rows, :], both_down[1, rows, :] = forward(opt.at[1], stacked)

        for p in range(2):
            both_up[p] = both_down[p].T

        @pl.loop(0, chunks // 2)
        def _(turn):
            down_first(2 * turn)
            down_first(2 * turn + 1)
            second_step(2 * turn, 2)

            @pl.when(z == last - 1)
            def _():
                prepare(2 * turn, 2)

        @pl.when(z < last - 1)
        def _():
            @pl.loop(0, chunks // 2)
            def _(turn):
                prepare(2 * turn, 2)

    @pl.when(z == last)
    def _():
        @pl.loop(0, lateral // 64)
        def _(block):
            rows = pl.ds(pl.multiple_of(block * 64, 64), 64)
            line = lax.broadcasted_iota(jnp.int32, (64, lateral), 0) + block * 64
            column = lax.broadcasted_iota(jnp.int32, (64, lateral), 1)
            unit = jnp.where(line == column, 1.0, 0.0).astype(F32)
            stacked = jnp.concatenate([unit.astype(BF16), jnp.zeros((64, lateral), BF16)], axis=0)
            real, imag = [part.astype(F32) for part in forward(opt.at[0], stacked)]
            cos_row, sin_row, model = cosines[1], sines[1], par[1, 1:2, :]
            real, imag = model * (cos_row * real - sin_row * imag), model * (cos_row * imag + sin_row * real)
            real, imag = back(opn.at[1], 1, real, imag)
            real, imag = back(opn.at[0], 0, real + par[0, 1:2, :] * unit, imag)
            both_down[0, rows, :], both_down[1, rows, :] = real.astype(BF16), imag.astype(BF16)

        def answer(place, n):
            for i in range(n):
                down_copy(place + i).wait_recv()
            finish(0, place, n, *forward(both_down, shift(0, place, n, *load(din, place, n))))

        def complete(place, n):
            second_step(place, n)
            nothing = jnp.zeros((n * SH, lateral), F32)
            source = source_of(1, place, n, nothing, nothing)
            source_of(0, place, n, *finish(1, place, n, *back(opn.at[1], 1, *source)))

        @pl.loop(0, (chunks - 2) // 2)
        def _(turn):
            answer(2 * turn, 2)
            complete(2 * turn, 2)

        answer(chunks - 2, 1)
        answer(chunks - 1, 1)
        complete(chunks - 2, 2)

    @pl.when((z > 0) & (z < last))
    def _():
        @pl.loop(0, chunks // 2)
        def _(turn):
            up_first(2 * turn)
            up_first(2 * turn + 1)
            up_rest(2 * turn, 2)

    @pl.when(z > 0)
    def _():
        share_gradient()

    @pl.when(z == 0)
    def _():
        def fetch(place):
            up_copy(place).wait_recv()
            up_copy(place + 1).wait_recv()
            return load(uin, place, 2)

        @pl.loop(0, chunks // 2 - 1)
        def _(turn):
            up(2 * turn, 2, *fetch(2 * turn))

        place = chunks - 2
        source = source_of(0, place, 2, *backward(1, place, 2, *fetch(place)))
        share_gradient()
        finish(0, place, 2, *back(opn.at[0], 0, *source))

    @pl.loop(1, n_freq)
    def _(k):
        source = (f + k) % n_freq
        pltpu.make_async_remote_copy(
            src_ref=gsend,
            dst_ref=gbox.at[source],
            send_sem=g_send.at[k],
            recv_sem=g_recv.at[source],
            device_id={"freq": source},
            device_id_type=MESH,
        ).wait_recv()

    total = jnp.sum(gbox[...], axis=0) * (1.0 / (2.0 * n_freq * SHOTS_DEV * n_freq))
    grad_ref[...] = jnp.concatenate([total[q : q + 1] for q in range(4)], axis=1)

    oper_copy(1 - c, c).wait_send()
    par_copy(c).wait_send()
    part_copy(1 - c, c).wait_send()

    @pl.loop(1, n_freq)
    def _(k):
        g_copy(k).wait_send()

    @pl.when(z == 0)
    def _():
        @pl.loop(1, n_freq)
        def _(k):
            box_copy(k).wait_send()

    @pl.loop(0, chunks)
    def _(place):
        @pl.when(z < last)
        def _():
            down_copy(place).wait_send()

        @pl.when(z > 0)
        def _():
            up_copy(place).wait_send()

        tops_here(c, place).wait()
        tops_there(1 - c, place, c).wait_send()
        tops_there(1 - c, place, 1 - c).wait_recv()


def body(traces, shot_of_trace, receiver_cell, slot_freq, operators, slowness, image_model):
    n_freq = lax.axis_size("freq")
    n_depth = lax.axis_size("depth")
    local_freqs = operators.shape[1]
    lateral = operators.shape[-1]
    shot_total = SHOTS_DEV * n_freq
    chunks = shot_total // SH
    block = (2, SH, lateral)
    vmem = pl.BlockSpec(memory_space=pltpu.VMEM)
    dma = pltpu.SemaphoreType.DMA
    gradient, tops = pl.pallas_call(
        functools.partial(kernel, n_depth, n_freq),
        out_shape=(
            jax.ShapeDtypeStruct((1, lateral), F32),
            jax.ShapeDtypeStruct((1, local_freqs, 2, shot_total, lateral), BF16),
        ),
        in_specs=[pl.BlockSpec(memory_space=pltpu.HBM)] * 7,
        out_specs=(vmem, vmem),
        scratch_shapes=[
            pltpu.SMEM(slot_freq.shape, jnp.int32),
            pltpu.VMEM(traces.shape, BF16),
            pltpu.VMEM(shot_of_trace.shape, jnp.int32),
            pltpu.VMEM(receiver_cell.shape, jnp.int32),
            pltpu.VMEM(slowness.shape, F32),
            pltpu.VMEM(image_model.shape, F32),
            pltpu.VMEM((2, 2, lateral, lateral), BF16),
            pltpu.VMEM((2, 2, lateral, lateral), BF16),
            pltpu.VMEM((2, lateral, lateral), BF16),
            pltpu.VMEM((2, lateral, lateral), BF16),
            pltpu.VMEM((chunks,) + block, F32),
            pltpu.VMEM((2, 8, lateral), F32),
            pltpu.VMEM((2, 1, lateral), F32),
            pltpu.VMEM((2, 1, lateral), F32),
            pltpu.VMEM((n_freq, 16, 128), BF16),
            pltpu.VMEM((n_freq, 16, 128), BF16),
            pltpu.VMEM((8, SH + 32, 128), F32),
            pltpu.VMEM((chunks,) + block, BF16),
            pltpu.VMEM((chunks,) + block, BF16),
            pltpu.VMEM((2, chunks) + block, BF16),
            pltpu.VMEM((chunks,) + block, BF16),
            pltpu.VMEM((2, chunks) + block, BF16),
            pltpu.VMEM((2, 8, lateral), F32),
            pltpu.VMEM((2, 4, 128), F32),
            pltpu.VMEM((2, 4, 128), F32),
            pltpu.VMEM((4, 128), F32),
            pltpu.VMEM((n_freq, 4, 128), F32),
            dma((7,)),
            dma(()),
            dma(()),
            dma(()),
            dma(()),
            dma((n_freq,)),
            dma((n_freq,)),
            dma((chunks,)),
            dma((chunks,)),
            dma((chunks,)),
            dma((chunks,)),
            dma((chunks,)),
            dma((chunks,)),
            dma((chunks,)),
            dma(()),
            dma(()),
            dma((n_freq,)),
            dma((n_freq,)),
        ],
        compiler_params=pltpu.CompilerParams(
            collective_id=0, has_side_effects=True, vmem_limit_bytes=48 * 2**20
        ),
        cost_estimate=pl.CostEstimate(flops=2 * 10**9, bytes_accessed=4 * 10**6, transcendentals=4096),
        name="migrate",
    )(
        *[
            pltpu.with_memory_space_constraint(given, pltpu.HBM)
            for given in (slot_freq, traces, shot_of_trace, receiver_cell, slowness, image_model, operators)
        ]
    )
    return gradient, tops


def solution(mesh):
    in_specs = (
        P("freq", None),
        P("freq", None),
        P("freq", None),
        P("freq"),
        P("depth", "freq", None, None, None),
        P("depth", None),
        P("depth", None),
    )
    out_specs = (P("depth", None), P("depth", "freq", None, None, None))
    return jax.shard_map(body, mesh=mesh, in_specs=in_specs, out_specs=out_specs, check_vma=False)
```

```python
import functools

import jax
import jax.numpy as jnp
from jax import lax
from jax.experimental import pallas as pl
from jax.experimental.pallas import tpu as pltpu
from jax.sharding import PartitionSpec as P

MESH = pl.DeviceIdType.MESH
SHOTS_DEV = 6
SH = 16
F32 = jnp.float32
BF16 = jnp.bfloat16


def product(rows, matrix):
    return jnp.dot(rows, matrix, preferred_element_type=F32)


def lanes(tile, row, width):
    return jnp.concatenate([tile[4 * q + row : 4 * q + row + 1] for q in range(width // 128)], axis=1)


def kernel(
    n_depth,
    n_freq,
    slot_hbm,
    traces_hbm,
    shot_hbm,
    cell_hbm,
    slow_hbm,
    model_hbm,
    oper_ref,
    grad_ref,
    tops_ref,
    slot_ref,
    traces_ref,
    shot_ref,
    cell_ref,
    slow_ref,
    model_ref,
    opn,
    opt,
    both_down,
    both_up,
    fixed,
    par,
    cosines,
    sines,
    outbox,
    inbox,
    bins,
    din,
    dout,
    vbuf,
    uin,
    abuf,
    gacc,
    gpart,
    gin,
    gsend,
    gbox,
    load_sem,
    oper_send,
    oper_recv,
    par_send,
    par_recv,
    box_send,
    box_recv,
    down_send,
    down_recv,
    up_send,
    up_recv,
    tops_local,
    tops_send,
    tops_recv,
    part_send,
    part_recv,
    g_send,
    g_recv,
):
    d = lax.axis_index("depth")
    f = lax.axis_index("freq")
    z = d // 2
    c = d % 2
    chunks = din.shape[0]
    lateral = din.shape[-1]
    last = n_depth // 2 - 1
    base = 2 * z
    partner = base + 1 - c

    def at(depth):
        return {"depth": depth}

    first_chunk = (f * SHOTS_DEV) // SH

    def chunk_of(place):
        return (first_chunk + place) % chunks

    below = (d + 2) % n_depth
    above = (d + n_depth - 2) % n_depth

    barrier = pltpu.get_barrier_semaphore()

    def greet(depth):
        pl.semaphore_signal(barrier, inc=1, device_id=at(depth), device_id_type=MESH)

    def greet_group(k):
        pl.semaphore_signal(barrier, inc=1, device_id={"freq": (f + k) % n_freq}, device_id_type=MESH)

    greet_group(n_freq // 2)

    @pl.loop(1, n_freq // 2)
    def _(k):
        greet_group(n_freq // 2 + k)
        greet_group(n_freq // 2 - k)

    greet(partner)

    @pl.when(z > 0)
    def _():
        greet(above)

    @pl.when(z < last)
    def _():
        greet(below)

    greeted = n_freq + jnp.where(z > 0, 1, 0) + jnp.where(z < last, 1, 0)

    loads = [
        pltpu.make_async_copy(source, target, load_sem.at[i])
        for i, (source, target) in enumerate(
            [
                (slow_hbm, slow_ref),
                (model_hbm, model_ref),
                (slot_hbm, slot_ref),
                (traces_hbm, traces_ref),
                (shot_hbm, shot_ref),
                (cell_hbm, cell_ref),
                (oper_ref.at[0, c], opn.at[c]),
            ]
        )
    ]

    @pl.when(z == 0)
    def _():
        for load in loads[3:6]:
            load.start()

    for load in loads[:3] + loads[6:]:
        load.start()
    for load in loads[:2]:
        load.wait()

    row8 = lax.broadcasted_iota(jnp.int32, (8, lateral), 0)
    par[c] = jnp.where(row8 == 0, slow_ref[...], model_ref[...])

    @pl.when(z == 0)
    def _():
        for load in loads[3:6]:
            load.wait()
        rows = n_freq * 16
        row = lax.broadcasted_iota(jnp.int32, (rows, 128), 0)
        column = lax.broadcasted_iota(jnp.int32, (rows, 128), 1)
        group, within = row // 16, row % 16
        kind, piece = within % 4, within // 4
        wanted = jnp.where(kind < 2, group * 4 + 2 * c + kind, -1)
        total = jnp.zeros((rows, 128), F32)
        for q in range(4):
            select = jnp.where((column == wanted) & (piece == q), 1.0, 0.0).astype(BF16)
            total += lax.dot_general(
                select,
                traces_ref[128 * q : 128 * (q + 1), :],
                (((1,), (1,)), ((), ())),
                preferred_element_type=F32,
            )
        cell = cell_ref[...]
        first = (cell // 128 * 8 + shot_ref[...]).astype(F32)
        second = (cell % 128).astype(F32)
        row16 = lax.broadcasted_iota(jnp.int32, (16, 128), 0)
        label = jnp.zeros((16, 128), F32)
        for q in range(4):
            label = jnp.where(row16 == 4 * q + 2, first[:, 128 * q : 128 * (q + 1)], label)
            label = jnp.where(row16 == 4 * q + 3, second[:, 128 * q : 128 * (q + 1)], label)
        filled = total.reshape(n_freq, 16, 128) + label[None]
        outbox[...] = filled.astype(BF16)
        inbox[f] = outbox[f]

    pl.semaphore_wait(barrier, greeted)

    def box_copy(k):
        return pltpu.make_async_remote_copy(
            src_ref=outbox.at[(f + k) % n_freq],
            dst_ref=inbox.at[f],
            send_sem=box_send.at[k],
            recv_sem=box_recv.at[f],
            device_id={"freq": (f + k) % n_freq},
            device_id_type=MESH,
        )

    @pl.when(z == 0)
    def _():
        @pl.loop(1, n_freq // 2)
        def _(k):
            box_copy(k).start()
            box_copy(n_freq - k).start()

        box_copy(n_freq // 2).start()

    def par_copy(index):
        return pltpu.make_async_remote_copy(
            src_ref=par.at[index],
            dst_ref=par.at[index],
            send_sem=par_send,
            recv_sem=par_recv,
            device_id=at(partner),
            device_id_type=MESH,
        )

    def oper_copy(slot, index):
        return pltpu.make_async_remote_copy(
            src_ref=oper_ref.at[0, slot],
            dst_ref=opn.at[index],
            send_sem=oper_send,
            recv_sem=oper_recv,
            device_id=at(partner),
            device_id_type=MESH,
        )

    oper_copy(1 - c, c).start()
    par_copy(c).start()

    loads[2].wait()
    loads[6].wait()
    scale = 0.1 * (slot_ref[c].astype(F32) + 1.0)

    def angles(e):
        theta = scale * par[e, 0:1, :]
        cosines[e] = jnp.cos(theta)
        sines[e] = jnp.sin(theta)

    gacc[...] = jnp.zeros_like(gacc)
    for p in range(2):
        opt[c, p] = opn[c, p].T
    par_copy(1 - c).wait_recv()
    angles(0)
    angles(1)
    oper_copy(c, 1 - c).wait_recv()

    for p in range(2):
        opt[1 - c, p] = opn[1 - c, p].T

    def wait_box(source):
        @pl.when(source != f)
        def _():
            pltpu.make_async_remote_copy(
                src_ref=outbox.at[source],
                dst_ref=inbox.at[source],
                send_sem=box_send.at[source],
                recv_sem=box_recv.at[source],
                device_id={"freq": source},
                device_id_type=MESH,
            ).wait_recv()

    counts = [(SH * j + SH - 1) // SHOTS_DEV - SH * j // SHOTS_DEV + 1 for j in range(chunks)]
    fewest, most = min(counts), max(counts)

    def bin_chunk(place):
        j = chunk_of(place)
        start = SH * j
        first_source = start // SHOTS_DEV
        fresh = jnp.where(place == 0, first_source, (start + SHOTS_DEV - 1) // SHOTS_DEV)
        after = jnp.where(
            (place == chunks - 1) & (first_chunk > 0),
            (SH * first_chunk) // SHOTS_DEV,
            (start + SH - 1) // SHOTS_DEV + 1,
        )

        @pl.loop(fresh, after)
        def _(source):
            wait_box(source)

        top = 8 + SHOTS_DEV * first_source - start
        row = lax.broadcasted_iota(jnp.int32, (32, 4 * 128), 0).astype(F32)
        lane_row = lax.broadcasted_iota(jnp.int32, (128, 4 * 128), 0).astype(F32)

        def add_source(i):
            tile = inbox[first_source + i].astype(F32)
            real, imag = lanes(tile, 0, 512), lanes(tile, 1, 512)
            first, low = lanes(tile, 2, 512), lanes(tile, 3, 512)
            hit = row == first
            left = jnp.concatenate(
                [jnp.where(hit, real, 0.0).astype(BF16), jnp.where(hit, imag, 0.0).astype(BF16)], axis=0
            )
            right = jnp.where(lane_row == low, 1.0, 0.0).astype(BF16)
            part = lax.dot_general(left, right, (((1,), (1,)), ((), ())), preferred_element_type=F32)
            for g in range(8):
                bins[g, pl.ds(top + SHOTS_DEV * i, 8), :] = part[8 * g : 8 * (g + 1)]

        for i in range(fewest):
            add_source(i)

        for i in range(fewest, most):

            @pl.when(first_source + i <= (start + SH - 1) // SHOTS_DEV)
            def _():
                add_source(i)

        for p in range(2):
            for high in range(4):
                din[place, p, :, 128 * high : 128 * (high + 1)] = bins[4 * p + high, 8 : 8 + SH, :].astype(BF16)

    def down_copy(place):
        return pltpu.make_async_remote_copy(
            src_ref=dout.at[place],
            dst_ref=din.at[place],
            send_sem=down_send.at[place],
            recv_sem=down_recv.at[place],
            device_id=at(below),
            device_id_type=MESH,
        )

    def up_copy(place):
        return pltpu.make_async_remote_copy(
            src_ref=abuf.at[0, place],
            dst_ref=uin.at[place],
            send_sem=up_send.at[place],
            recv_sem=up_recv.at[place],
            device_id=at(above),
            device_id_type=MESH,
        )

    def load(ref, place, n):
        return [ref[pl.ds(place, n), p].reshape(n * SH, lateral).astype(F32) for p in range(2)]

    def store(ref, place, n, real, imag):
        ref[pl.ds(place, n), 0] = real.reshape(n, SH, lateral)
        ref[pl.ds(place, n), 1] = imag.reshape(n, SH, lateral)

    def shift(e, place, n, real, imag):
        cos_row, sin_row = cosines[e], sines[e]
        shifted_real = (cos_row * real - sin_row * imag).astype(BF16)
        shifted_imag = (cos_row * imag + sin_row * real).astype(BF16)
        store(vbuf.at[e], place, n, shifted_real, shifted_imag)
        return jnp.concatenate([shifted_real, shifted_imag], axis=0)

    def forward(table, stacked):
        rows = stacked.shape[0] // 2
        by_real, by_imag = product(stacked, table[0]), product(stacked, table[1])
        return (by_real[:rows] - by_imag[rows:]).astype(BF16), (by_imag[:rows] + by_real[rows:]).astype(BF16)

    def down(place, n):
        stacked = shift(0, place, n, *load(din, place, n))
        real, imag = forward(opt.at[0], stacked)
        stacked = shift(1, place, n, real.astype(F32), imag.astype(F32))
        real, imag = forward(opt.at[1], stacked)
        store(dout, place, n, real, imag)
        for i in range(n):
            down_copy(place + i).start()

    def down_first(place):
        down_copy(place).wait_recv()
        stacked = shift(0, place, 1, *load(din, place, 1))
        store(dout, place, 1, *forward(both_down, stacked))
        down_copy(place).start()

    def second_step(place, n):
        stacked = jnp.concatenate([part.astype(BF16) for part in load(vbuf.at[0], place, n)], axis=0)
        real, imag = forward(opt.at[0], stacked)
        shift(1, place, n, real.astype(F32), imag.astype(F32))

    def rows_of(place):
        return pl.ds(pl.multiple_of(chunk_of(place) * SH, SH), SH)

    def tops_here(e, place):
        return pltpu.make_async_copy(abuf.at[e, place], tops_ref.at[0, c, :, rows_of(place), :], tops_local.at[place])

    def tops_there(e, place, its_slot):
        return pltpu.make_async_remote_copy(
            src_ref=abuf.at[e, place],
            dst_ref=tops_ref.at[0, its_slot, :, rows_of(place), :],
            send_sem=tops_send.at[place],
            recv_sem=tops_recv.at[place],
            device_id=at(partner),
            device_id_type=MESH,
        )

    def back(table, e, real, imag):
        rows = real.shape[0]
        stacked = jnp.concatenate([real.astype(BF16), imag.astype(BF16)], axis=0)
        by_real, by_imag = product(stacked, table[0]), product(stacked, table[1])
        back_real = by_real[:rows] + by_imag[rows:]
        back_imag = by_real[rows:] - by_imag[:rows]
        cos_row, sin_row = cosines[e], sines[e]
        return cos_row * back_real + sin_row * back_imag, cos_row * back_imag - sin_row * back_real

    def source_of(e, place, n, real, imag):
        old_real, old_imag = load(vbuf.at[e], place, n)
        model = par[e, 1:2, :]
        source_real = real + model * old_real
        source_imag = imag + model * old_imag
        term = old_real * source_real + old_imag * source_imag
        gacc[e] += jnp.sum(term.reshape(n * SH // 8, 8, lateral), axis=0)
        return source_real, source_imag

    def finish(e, place, n, real, imag):
        real, imag = real.astype(BF16), imag.astype(BF16)
        store(abuf.at[e], place, n, real, imag)
        for i in range(n):
            if e == 0:

                @pl.when(z > 0)
                def _():
                    up_copy(place + i).start()

            @pl.when(c == e)
            def _():
                tops_here(e, place + i).start()

            @pl.when(c != e)
            def _():
                tops_there(e, place + i, c).start()

        return real.astype(F32), imag.astype(F32)

    def backward(e, place, n, real, imag):
        return finish(e, place, n, *back(opn.at[e], e, *source_of(e, place, n, real, imag)))

    def prepare(place, n):
        old_real, old_imag = load(vbuf.at[0], place, n)
        model = par[0, 1:2, :]
        store(fixed, place, n, *back(opn.at[0], 0, model * old_real, model * old_imag))

    def up_first(place):
        up_copy(place).wait_recv()
        real, imag = source_of(1, place, 1, *load(uin, place, 1))
        store(uin, place, 1, real.astype(BF16), imag.astype(BF16))
        fixed_real, fixed_imag = load(fixed, place, 1)
        top_real, top_imag = back(both_up, 0, real, imag)
        finish(0, place, 1, top_real + fixed_real, top_imag + fixed_imag)

    def up_rest(place, n):
        source_of(0, place, n, *finish(1, place, n, *back(opn.at[1], 1, *load(uin, place, n))))

    def up(place, n, real, imag):
        real, imag = backward(1, place, n, real, imag)
        backward(0, place, n, real, imag)

    row4 = lax.broadcasted_iota(jnp.int32, (4, 128), 0)

    def rows_tile(summed):
        tile = jnp.zeros((4, 128), F32)
        for q in range(4):
            tile = jnp.where(row4 == q, summed[:, 128 * q : 128 * (q + 1)], tile)
        return tile

    def part_copy(e, sender):
        return pltpu.make_async_remote_copy(
            src_ref=gpart.at[e],
            dst_ref=gin.at[sender],
            send_sem=part_send,
            recv_sem=part_recv,
            device_id=at(partner),
            device_id_type=MESH,
        )

    def g_copy(k):
        return pltpu.make_async_remote_copy(
            src_ref=gsend,
            dst_ref=gbox.at[f],
            send_sem=g_send.at[k],
            recv_sem=g_recv.at[f],
            device_id={"freq": (f + k) % n_freq},
            device_id_type=MESH,
        )

    def share_gradient():
        for e in range(2):
            gpart[e] = rows_tile(jnp.sum(gacc[e], axis=0, keepdims=True))

            @pl.when(c != e)
            def _():
                part_copy(e, c).start()

        part_copy(0, 1 - c).wait_recv()
        total = gpart[c] + gin[1 - c]
        gsend[...] = total
        gbox[f] = total

        @pl.loop(1, n_freq)
        def _(k):
            g_copy(k).start()

    @pl.when(z == 0)
    def _():
        bin_chunk(0)
        down(0, 1)

        @pl.loop(0, (chunks - 2) // 2)
        def _(turn):
            place = 1 + 2 * turn
            bin_chunk(place)
            bin_chunk(place + 1)
            down(place, 2)

        bin_chunk(chunks - 1)
        down(chunks - 1, 1)

    @pl.when((z > 0) & (z < last))
    def _():
        @pl.loop(0, lateral // 64)
        def _(block):
            rows = pl.ds(pl.multiple_of(block * 64, 64), 64)
            real, imag = opt[0, 0, rows, :].astype(F32), opt[0, 1, rows, :].astype(F32)
            cos_row, sin_row = cosines[1], sines[1]
            stacked = jnp.concatenate(
                [(cos_row * real - sin_row * imag).astype(BF16), (cos_row * imag + sin_row * real).astype(BF16)],
                axis=0,
            )
            both_down[0, rows, :], both_down[1, rows, :] = forward(opt.at[1], stacked)

        for p in range(2):
            both_up[p] = both_down[p].T

        @pl.loop(0, chunks // 2)
        def _(turn):
            down_first(2 * turn)
            down_first(2 * turn + 1)
            second_step(2 * turn, 2)

            @pl.when(z == last - 1)
            def _():
                prepare(2 * turn, 2)

        @pl.when(z < last - 1)
        def _():
            @pl.loop(0, chunks // 2)
            def _(turn):
                prepare(2 * turn, 2)

    @pl.when(z == last)
    def _():
        @pl.loop(0, lateral // 64)
        def _(block):
            rows = pl.ds(pl.multiple_of(block * 64, 64), 64)
            line = lax.broadcasted_iota(jnp.int32, (64, lateral), 0) + block * 64
            column = lax.broadcasted_iota(jnp.int32, (64, lateral), 1)
            unit = jnp.where(line == column, 1.0, 0.0).astype(F32)
            stacked = jnp.concatenate([unit.astype(BF16), jnp.zeros((64, lateral), BF16)], axis=0)
            real, imag = [part.astype(F32) for part in forward(opt.at[0], stacked)]
            cos_row, sin_row, model = cosines[1], sines[1], par[1, 1:2, :]
            real, imag = model * (cos_row * real - sin_row * imag), model * (cos_row * imag + sin_row * real)
            real, imag = back(opn.at[1], 1, real, imag)
            real, imag = back(opn.at[0], 0, real + par[0, 1:2, :] * unit, imag)
            both_down[0, rows, :], both_down[1, rows, :] = real.astype(BF16), imag.astype(BF16)

        def answer(place, n):
            for i in range(n):
                down_copy(place + i).wait_recv()
            finish(0, place, n, *forward(both_down, shift(0, place, n, *load(din, place, n))))

        def complete(place, n):
            second_step(place, n)
            nothing = jnp.zeros((n * SH, lateral), F32)
            source = source_of(1, place, n, nothing, nothing)
            source_of(0, place, n, *finish(1, place, n, *back(opn.at[1], 1, *source)))

        @pl.loop(0, (chunks - 2) // 2)
        def _(turn):
            answer(2 * turn, 1)
            answer(2 * turn + 1, 1)
            complete(2 * turn, 2)

        answer(chunks - 2, 1)
        answer(chunks - 1, 1)
        complete(chunks - 2, 2)

    @pl.when((z > 0) & (z < last))
    def _():
        @pl.loop(0, chunks // 2)
        def _(turn):
            up_first(2 * turn)
            up_first(2 * turn + 1)
            up_rest(2 * turn, 2)

    @pl.when(z > 0)
    def _():
        share_gradient()

    @pl.when(z == 0)
    def _():
        def fetch(place):
            up_copy(place).wait_recv()
            up_copy(place + 1).wait_recv()
            return load(uin, place, 2)

        @pl.loop(0, chunks // 2 - 1)
        def _(turn):
            up(2 * turn, 2, *fetch(2 * turn))

        place = chunks - 2
        source = source_of(0, place, 2, *backward(1, place, 2, *fetch(place)))
        share_gradient()
        finish(0, place, 2, *back(opn.at[0], 0, *source))

    @pl.loop(1, n_freq)
    def _(k):
        source = (f + k) % n_freq
        pltpu.make_async_remote_copy(
            src_ref=gsend,
            dst_ref=gbox.at[source],
            send_sem=g_send.at[k],
            recv_sem=g_recv.at[source],
            device_id={"freq": source},
            device_id_type=MESH,
        ).wait_recv()

    total = jnp.sum(gbox[...], axis=0) * (1.0 / (2.0 * n_freq * SHOTS_DEV * n_freq))
    grad_ref[...] = jnp.concatenate([total[q : q + 1] for q in range(4)], axis=1)

    oper_copy(1 - c, c).wait_send()
    par_copy(c).wait_send()
    part_copy(1 - c, c).wait_send()

    @pl.loop(1, n_freq)
    def _(k):
        g_copy(k).wait_send()

    @pl.when(z == 0)
    def _():
        @pl.loop(1, n_freq)
        def _(k):
            box_copy(k).wait_send()

    @pl.loop(0, chunks)
    def _(place):
        @pl.when(z < last)
        def _():
            down_copy(place).wait_send()

        @pl.when(z > 0)
        def _():
            up_copy(place).wait_send()

        tops_here(c, place).wait()
        tops_there(1 - c, place, c).wait_send()
        tops_there(1 - c, place, 1 - c).wait_recv()


def body(traces, shot_of_trace, receiver_cell, slot_freq, operators, slowness, image_model):
    n_freq = lax.axis_size("freq")
    n_depth = lax.axis_size("depth")
    local_freqs = operators.shape[1]
    lateral = operators.shape[-1]
    shot_total = SHOTS_DEV * n_freq
    chunks = shot_total // SH
    block = (2, SH, lateral)
    vmem = pl.BlockSpec(memory_space=pltpu.VMEM)
    dma = pltpu.SemaphoreType.DMA
    gradient, tops = pl.pallas_call(
        functools.partial(kernel, n_depth, n_freq),
        out_shape=(
            jax.ShapeDtypeStruct((1, lateral), F32),
            jax.ShapeDtypeStruct((1, local_freqs, 2, shot_total, lateral), BF16),
        ),
        in_specs=[pl.BlockSpec(memory_space=pltpu.HBM)] * 7,
        out_specs=(vmem, vmem),
        scratch_shapes=[
            pltpu.SMEM(slot_freq.shape, jnp.int32),
            pltpu.VMEM(traces.shape, BF16),
            pltpu.VMEM(shot_of_trace.shape, jnp.int32),
            pltpu.VMEM(receiver_cell.shape, jnp.int32),
            pltpu.VMEM(slowness.shape, F32),
            pltpu.VMEM(image_model.shape, F32),
            pltpu.VMEM((2, 2, lateral, lateral), BF16),
            pltpu.VMEM((2, 2, lateral, lateral), BF16),
            pltpu.VMEM((2, lateral, lateral), BF16),
            pltpu.VMEM((2, lateral, lateral), BF16),
            pltpu.VMEM((chunks,) + block, F32),
            pltpu.VMEM((2, 8, lateral), F32),
            pltpu.VMEM((2, 1, lateral), F32),
            pltpu.VMEM((2, 1, lateral), F32),
            pltpu.VMEM((n_freq, 16, 128), BF16),
            pltpu.VMEM((n_freq, 16, 128), BF16),
            pltpu.VMEM((8, SH + 32, 128), F32),
            pltpu.VMEM((chunks,) + block, BF16),
            pltpu.VMEM((chunks,) + block, BF16),
            pltpu.VMEM((2, chunks) + block, BF16),
            pltpu.VMEM((chunks,) + block, BF16),
            pltpu.VMEM((2, chunks) + block, BF16),
            pltpu.VMEM((2, 8, lateral), F32),
            pltpu.VMEM((2, 4, 128), F32),
            pltpu.VMEM((2, 4, 128), F32),
            pltpu.VMEM((4, 128), F32),
            pltpu.VMEM((n_freq, 4, 128), F32),
            dma((7,)),
            dma(()),
            dma(()),
            dma(()),
            dma(()),
            dma((n_freq,)),
            dma((n_freq,)),
            dma((chunks,)),
            dma((chunks,)),
            dma((chunks,)),
            dma((chunks,)),
            dma((chunks,)),
            dma((chunks,)),
            dma((chunks,)),
            dma(()),
            dma(()),
            dma((n_freq,)),
            dma((n_freq,)),
        ],
        compiler_params=pltpu.CompilerParams(
            collective_id=0, has_side_effects=True, vmem_limit_bytes=48 * 2**20
        ),
        cost_estimate=pl.CostEstimate(flops=2 * 10**9, bytes_accessed=4 * 10**6, transcendentals=4096),
        name="migrate",
    )(
        *[
            pltpu.with_memory_space_constraint(given, pltpu.HBM)
            for given in (slot_freq, traces, shot_of_trace, receiver_cell, slowness, image_model, operators)
        ]
    )
    return gradient, tops


def solution(mesh):
    in_specs = (
        P("freq", None),
        P("freq", None),
        P("freq", None),
        P("freq"),
        P("depth", "freq", None, None, None),
        P("depth", None),
        P("depth", None),
    )
    out_specs = (P("depth", None), P("depth", "freq", None, None, None))
    return jax.shard_map(body, mesh=mesh, in_specs=in_specs, out_specs=out_specs, check_vma=False)
```
